32 devices in a mesh: tm: 2 (over x), heads: 4 (over y, core), rep: 4 (over z).
Axes of the slice: x: 2, y: 2, z: 4, core: 2. Of those that a mesh axis runs over, the one named last changes fastest.
Arguments:
- queries: bfloat16 [2048, 2560], P(('tm', 'rep'), 'heads'), may hold values from -100 to 100
- keys: bfloat16 [2048, 2560], P(('tm', 'rep'), 'heads'), may hold values from -4 to 4
- values: bfloat16 [2048, 2560], P(('tm', 'rep'), 'heads'), may hold values from -6 to 6
- block_lists: int32 [16, 16], P(('tm', 'rep')), may hold values from 0 to 15, as said below
- list_counts: int32 [16], P(('tm', 'rep')), may hold values from 2 to 16, as said below
- out_weight: bfloat16 [2560, 5120], P('heads', 'rep'), may hold values from -0.125 to 0.125
- gate: float32 [5120], P('rep'), may hold values from 0.5 to 2
Outputs:
- branch: bfloat16 [2048, 5120], P(('tm', 'heads'), 'rep')
The draws below stay inside these ranges and needn't reach their ends.
Inputs may be any that keep to these rules, and one draw needn't show every extreme that they name: `block_lists`: entry 0 of block b's list is b itself; only the first list_counts[b] entries count, the rest are arbitrary block numbers. `list_counts`: every draw has a block whose count is 16.
All inputs are finite; a program needn't handle non-finite values.
Results may differ from the reference program's by a relative error of at most 0.0085.
Values may be sent and summed in bfloat16 or wider, within the bound.
A program may use at most 64 MiB of HBM per device.

```python
import math
import jax
import jax.numpy as jnp
from jax import lax

D = 5120
HD = 128
HEADS = 20
BLOCK = 128
LIST = 16
TOKENS = 2048
QBLOCKS = 16
FRAMES = 2
FRAME_BLOCKS = 8


def list_draw(key):
    base = jax.random.fold_in(key, 23)
    key_dist, key_sign, key_space = jax.random.split(base, 3)
    block_ids = jnp.arange(QBLOCKS, dtype=jnp.int32)
    frame = block_ids // FRAME_BLOCKS
    tries = jax.random.randint(key_dist, (QBLOCKS, LIST, 3), 0, FRAMES)
    distance = jnp.min(tries, axis=2)
    direction = 2 * jax.random.randint(key_sign, (QBLOCKS, LIST), 0, 2) - 1
    target = frame[:, None] + direction * distance
    outside = (target < 0) | (target >= FRAMES)
    target = jnp.where(outside, frame[:, None] - direction * distance, target)
    target = jnp.clip(target, 0, FRAMES - 1)
    spatial = jax.random.randint(key_space, (QBLOCKS, LIST), 0, FRAME_BLOCKS)
    listed = target * FRAME_BLOCKS + spatial
    first_slot = jnp.arange(LIST)[None, :] == 0
    listed = jnp.where(first_slot, block_ids[:, None], listed)
    return listed.astype(jnp.int32)


def count_draw(key):
    base = jax.random.fold_in(key, 31)
    key_frame, key_block, key_pick = jax.random.split(base, 3)
    frame_shift = jax.random.randint(key_frame, (FRAMES,), 0, 3)
    block_shift = jax.random.randint(key_block, (QBLOCKS,), 0, 2)
    block_ids = jnp.arange(QBLOCKS, dtype=jnp.int32)
    shift_total = jnp.minimum(frame_shift[block_ids // FRAME_BLOCKS] + block_shift, 2)
    counts = jnp.maximum(jnp.right_shift(jnp.int32(LIST), shift_total), 2)
    chosen = jax.random.randint(key_pick, (), 0, QBLOCKS)
    counts = jnp.where(block_ids == chosen, LIST, counts)
    return counts.astype(jnp.int32)


def paired_fields(key):
    base = jax.random.fold_in(key, 11)
    key_query, key_key = jax.random.split(base, 2)
    width = HEADS * HD
    key_field = jnp.clip(jax.random.normal(key_key, (TOKENS, width), jnp.float32), -4.0, 4.0)
    query_field = jnp.clip(2.0 * jax.random.normal(key_query, (TOKENS, width), jnp.float32), -8.0, 8.0)
    return (query_field, key_field)


def draw_queries(key, part):
    return paired_fields(key)[0].astype(jnp.bfloat16)


def draw_keys(key, part):
    return paired_fields(key)[1].astype(jnp.bfloat16)


def draw_block_lists(key, part):
    return list_draw(key)


def draw_list_counts(key, part):
    return count_draw(key)


def shard_levels(key, dims, cuts, smallest, top_value):
    gain = 1.0
    for axis_at, parts in cuts:
        heights = jax.random.uniform(jax.random.fold_in(jax.random.fold_in(key, 6), axis_at), (parts,), jnp.float32, smallest / len(cuts), top_value / len(cuts))
        gain = gain * jnp.repeat(jnp.exp(heights), dims[axis_at] // parts).reshape((-1,) + (1,) * (len(dims) - 1 - axis_at))
    return gain


def normal_values(own_key, shape, spread, bound, pieces=(), held_as=jnp.bfloat16):
    entries = spread * jax.random.normal(own_key, shape, jnp.float32)
    if pieces:
        entries = entries * shard_levels(own_key, shape, pieces, -0.22, 0.18)
    return jnp.clip(entries, -bound, bound).astype(held_as)


def setup_inputs(seed: int = 0) -> dict:
    key_of = jax.random.split(jax.random.key(seed), 8)
    return {
        "queries": draw_queries(jax.random.fold_in(key_of[7], 71), 0),
        "keys": draw_keys(jax.random.fold_in(key_of[7], 71), 0),
        "values": normal_values(key_of[2], (TOKENS, HEADS * HD), 1.0, 6.0, ((0, 8), (1, 4))),
        "block_lists": draw_block_lists(jax.random.fold_in(key_of[7], 71), 0),
        "list_counts": draw_list_counts(jax.random.fold_in(key_of[7], 71), 0),
        "out_weight": normal_values(key_of[5], (HEADS * HD, D), (HEADS * HD) ** -0.5, 0.125, ((0, 4), (1, 4))),
        "gate": jnp.clip(jnp.exp(math.log(2.0) - 1.3862944 * jax.random.uniform(key_of[6], (D,), jnp.float32) ** shard_levels(key_of[6], (D,), ((0, 4),), -0.2, 0.2)), 0.5, 2.0),
    }


def reference(queries, keys, values, block_lists, list_counts, out_weight, gate):
    slot_ids = jnp.arange(LIST)
    slot_used = slot_ids[None, :] < list_counts[:, None]
    repeated = (block_lists[:, :, None] == block_lists[:, None, :]) & slot_used[:, None, :] & (slot_ids[None, None, :] < slot_ids[None, :, None])
    fresh = slot_used & jnp.logical_not(jnp.any(repeated, axis=2))
    logit_scale = 1.0 / (HD ** 0.5)

    def one_head(head_index):
        start = (head_index * HD).astype(jnp.int32)
        head_queries = lax.dynamic_slice_in_dim(queries, start, HD, 1).reshape(QBLOCKS, BLOCK, HD).astype(jnp.float32)
        key_head = lax.dynamic_slice_in_dim(keys, start, HD, 1).reshape(QBLOCKS, BLOCK, HD)
        value_head = lax.dynamic_slice_in_dim(values, start, HD, 1).reshape(QBLOCKS, BLOCK, HD)
        gathered_keys = key_head[block_lists].astype(jnp.float32)
        gathered_values = value_head[block_lists].astype(jnp.float32)
        attention_logits = jnp.einsum("zsh,zgyh->zsgy", head_queries, gathered_keys, precision=lax.Precision.HIGHEST) * logit_scale
        masked = jnp.where(fresh[:, None, :, None], attention_logits, -jnp.inf)
        row_max = jnp.max(masked, axis=(2, 3), keepdims=True)
        weights = jnp.exp(masked - row_max)
        denom = jnp.sum(weights, axis=(2, 3))
        rounded_output = lax.optimization_barrier(weights.astype(jnp.bfloat16)).astype(jnp.float32)
        weighted_value_sum = jnp.einsum("pwfh,pfhi->pwi", rounded_output, gathered_values, precision=lax.Precision.HIGHEST)
        return (weighted_value_sum / denom[:, :, None]).reshape(TOKENS, HD)

    per_head = lax.map(one_head, jnp.arange(HEADS, dtype=jnp.int32))
    attended = jnp.transpose(per_head, (1, 0, 2)).reshape(TOKENS, HEADS * HD).astype(jnp.bfloat16)
    projected = jnp.dot(attended, out_weight, preferred_element_type=jnp.float32)
    return (gate.astype(jnp.float32)[None, :] * projected).astype(jnp.bfloat16)
```

```python
import functools

import jax
import jax.numpy as jnp
from jax import lax
from jax.experimental import pallas as pl
from jax.experimental.pallas import tpu as pltpu
from jax.sharding import PartitionSpec as P

HD = 128
BLOCK = 128
LIST = 16
NEG = 1e30
MESH = pl.DeviceIdType.MESH


def extra_rep(g, reps):
    half = g // 2
    return ((1 - g % 2) * half + (g % 2) * (reps - 1 - half)) % reps


def kernel(
    dims,
    q_ref, k_ref, v_ref, lists_ref, counts_ref, w_ref, gate_ref,
    out_ref,
    qbuf, kbuf, vbuf, mbuf, stage, abuf, wbuf, acc,
    zs, zr, zms, zmr, xs, xr, own_sem, w_own, ats, atr, gs, gr, wys, wyr, wms, wmr,
):
    frames, groups, reps, toks, heads, base, extra, slots, plane_heads = dims
    tm = lax.axis_index("tm")
    g = lax.axis_index("heads")
    z = lax.axis_index("rep")
    span = reps * toks
    local_blocks = toks // BLOCK
    frame_blocks = span // BLOCK
    lanes = mbuf.shape[-1]

    def cols(head):
        return pl.ds(pl.multiple_of(head * HD, HD), HD)

    def rows(rep):
        return pl.ds(pl.multiple_of(rep * toks, toks), toks)

    def extra_rank(plane, group):
        return sum(
            jnp.where((other < group) & ((plane - extra_rep(other, reps) + reps) % reps < extra), 1, 0)
            for other in range(groups)
        )

    def extra_of(group):
        return (z - extra_rep(group, reps) + reps) % reps

    my_extra = extra_of(g)
    has_extra = my_extra < extra

    def place(group, head):
        if head < base * reps:
            return head % reps, (head // reps) * groups + group
        plane = (extra_rep(group, reps) + head - base * reps) % reps
        return plane, base * groups + extra_rank(plane, group)

    barrier = pltpu.get_barrier_semaphore()
    for axis, count, me in (("rep", reps, z), ("tm", frames, tm), ("heads", groups, g)):
        for d in range(1, count):
            pl.semaphore_signal(
                barrier, inc=1, device_id={axis: (me + d) % count}, device_id_type=MESH
            )
    pl.semaphore_wait(barrier, reps + frames + groups - 3)

    row_id = lax.broadcasted_iota(jnp.int32, (8, lanes), 0)
    lane_id = lax.broadcasted_iota(jnp.int32, (8, lanes), 1)
    allowed = jnp.zeros((8, lanes), jnp.float32)
    for b in range(local_blocks):
        used = counts_ref[b]
        for j in range(LIST):
            hit = (lane_id == lists_ref[b, j]) & (row_id == b) & (jnp.full((8, lanes), j) < used)
            allowed = jnp.where(hit, 1.0, allowed)
    mbuf[z] = allowed

    def mask_copy(dst, src):
        return pltpu.make_async_remote_copy(
            src_ref=mbuf.at[src], dst_ref=mbuf.at[src],
            send_sem=zms.at[dst], recv_sem=zmr.at[src],
            device_id={"rep": dst}, device_id_type=MESH,
        )

    sources = (k_ref, v_ref, q_ref)

    def landing(kind, slot, rep):
        if kind == 2:
            return qbuf.at[slot, rows(rep)]
        return (kbuf, vbuf)[kind].at[slot, tm, rows(rep)]

    def z_copy(kind, slot, head, dst, src):
        return pltpu.make_async_remote_copy(
            src_ref=sources[kind].at[:, cols(head)], dst_ref=landing(kind, slot, src),
            send_sem=zs.at[kind, slot, dst], recv_sem=zr.at[kind, slot, src],
            device_id={"rep": dst}, device_id_type=MESH,
        )

    def own_copy(kind, slot, head):
        return pltpu.make_async_copy(
            sources[kind].at[:, cols(head)], landing(kind, slot, z), own_sem.at[kind, slot]
        )

    def x_copy(kind, slot, rep, d, src=None):
        there = landing(kind, slot, rep)
        return pltpu.make_async_remote_copy(
            src_ref=there if src is None else src, dst_ref=there,
            send_sem=xs.at[kind, slot, rep, d - 1], recv_sem=xr.at[kind, slot, rep, d - 1],
            device_id={"tm": (tm + d) % frames}, device_id_type=MESH,
        )

    def my_head(slot):
        return slot * reps + z if slot < base else base * reps + my_extra

    def each_slot(act):
        for slot in range(base):
            act(slot)
        if extra:
            pl.when(has_extra)(lambda: act(base))

    for d in range(1, reps):
        mask_copy((z + d) % reps, z).start()
    for kind in range(3):
        for d in range(1, reps):
            dst = (z + d) % reps
            for slot in range(base):
                z_copy(kind, slot, slot * reps + dst, dst, z).start()
        for n in range(extra):
            dst = (extra_rep(g, reps) + n) % reps

            @pl.when(dst != z)
            def _():
                z_copy(kind, base, base * reps + n, dst, z).start()

        def start_own(slot):
            own_copy(kind, slot, my_head(slot)).start()
            if kind < 2:
                for d in range(1, frames):
                    x_copy(kind, slot, z, d, sources[kind].at[:, cols(my_head(slot))]).start()

        each_slot(start_own)

    mate = g + 1 - 2 * (g % 2)

    def w_there(group, head):
        plane, at = place(group, head)
        return wbuf.at[plane, cols(at)]

    def w_far(k, head):
        return pltpu.make_async_remote_copy(
            src_ref=w_ref.at[pl.ds(head * HD, HD)], dst_ref=w_there(g, head),
            send_sem=wys.at[k - 1, head], recv_sem=wyr.at[k - 1, head],
            device_id={"heads": (g + 2 * k) % groups}, device_id_type=MESH,
        )

    def w_mate(k, head):
        from_group = (g - 2 * k + groups) % groups
        there = w_there(from_group, head)
        return pltpu.make_async_remote_copy(
            src_ref=there if k else w_ref.at[pl.ds(head * HD, HD)], dst_ref=there,
            send_sem=wms.at[k, head], recv_sem=wmr.at[k, head],
            device_id={"heads": mate}, device_id_type=MESH,
        )

    def w_local(head):
        return pltpu.make_async_copy(
            w_ref.at[pl.ds(head * HD, HD)], w_there(g, head), w_own.at[head]
        )

    halves = groups // 2
    for head in range(heads):
        for k in range(1, halves):
            w_far(k, head).start()
    for head in range(heads):
        w_mate(0, head).start()
        w_local(head).start()

    for kind in range(2):
        for d in range(1, reps):
            src = (z + d) % reps

            def pass_on(slot):
                z_copy(kind, slot, 0, z, src).wait_recv()
                for e in range(1, frames):
                    x_copy(kind, slot, src, e).start()

            each_slot(pass_on)
    for d in range(1, reps):
        mask_copy(z, (z + d) % reps).wait_recv()

    def rest(slot):
        for kind in range(3):
            own_copy(kind, slot, my_head(slot)).wait()
        for kind in range(2):
            for rep in range(reps):
                for d in range(1, frames):
                    there = (kbuf, vbuf)[kind].at[slot, (tm - d + frames) % frames, rows(rep)]
                    pltpu.make_async_remote_copy(
                        src_ref=there, dst_ref=there,
                        send_sem=xs.at[kind, slot, rep, d - 1],
                        recv_sem=xr.at[kind, slot, rep, d - 1],
                        device_id={"tm": (tm + d) % frames}, device_id_type=MESH,
                    ).wait_recv()

    each_slot(rest)

    def attend(slot, chunk):
        queries = qbuf[slot, rows(chunk)]
        mask_rows = mbuf[chunk].astype(jnp.bfloat16)
        block_of = lax.broadcasted_iota(jnp.int32, (lanes, span), 1) // BLOCK
        lane_of = lax.broadcasted_iota(jnp.int32, (lanes, span), 0)
        factor = 1.4426950408889634 / HD**0.5

        def step(frame, state):
            top, total, sums = state
            spread = jnp.where(block_of + frame * frame_blocks == lane_of, 1.0, 0.0)
            bias = NEG * (
                jnp.dot(mask_rows, spread.astype(jnp.bfloat16), preferred_element_type=jnp.float32)
                - 1.0
            )
            scores = lax.dot_general(
                queries, kbuf[slot, frame], (((1,), (1,)), ((), ())),
                preferred_element_type=jnp.float32,
            )
            scores = scores + jnp.concatenate(
                [jnp.broadcast_to(bias[b : b + 1], (BLOCK, span)) for b in range(local_blocks)], 0
            )
            new_top = jnp.maximum(top, jnp.max(scores, axis=1, keepdims=True))
            weights = jnp.exp2((scores - new_top) * factor)
            scale = jnp.exp2((top - new_top) * factor)
            total = total * scale + jnp.sum(weights, axis=1, keepdims=True)
            sums = sums * scale + jnp.dot(
                weights.astype(jnp.bfloat16), vbuf[slot, frame], preferred_element_type=jnp.float32
            )
            return new_top, total, sums

        state = (
            jnp.full((toks, 1), -NEG, jnp.float32),
            jnp.zeros((toks, 1), jnp.float32),
            jnp.zeros((toks, HD), jnp.float32),
        )
        _, total, sums = lax.fori_loop(0, frames, step, state, unroll=min(frames, 2))
        stage[slot, rows(chunk)] = (sums / total).astype(jnp.bfloat16)

    def position(slot, group):
        return slot * groups + group if slot < base else base * groups + extra_rank(z, group)

    def att_copy(slot, chunk):
        return pltpu.make_async_remote_copy(
            src_ref=stage.at[slot, rows(chunk)], dst_ref=abuf.at[z, :, cols(position(slot, g))],
            send_sem=ats.at[slot, chunk], recv_sem=atr.at[slot, g],
            device_id={"heads": chunk}, device_id_type=MESH,
        )

    def att_local(slot):
        return pltpu.make_async_copy(
            stage.at[slot, rows(g)], abuf.at[z, :, cols(position(slot, g))], ats.at[slot, g]
        )

    def one_chunk(i, _):
        chunk = (z + i) % reps

        def work(slot):
            @pl.when(i > 0)
            def _():
                z_copy(2, slot, 0, z, chunk).wait_recv()

            attend(slot, chunk)

            @pl.when(chunk != g)
            def _():
                att_copy(slot, chunk).start()

            @pl.when(chunk == g)
            def _():
                att_local(slot).start()

        each_slot(work)
        return 0

    lax.fori_loop(0, reps, one_chunk, 0)

    each_slot(lambda slot: att_local(slot).wait())
    for d in range(1, groups):
        other = (g + d) % groups

        def arrive(slot):
            there = abuf.at[z, :, cols(position(slot, other))]
            pltpu.make_async_remote_copy(
                src_ref=stage.at[slot, rows(g)], dst_ref=there,
                send_sem=ats.at[slot, other], recv_sem=atr.at[slot, other],
                device_id={"heads": other}, device_id_type=MESH,
            ).wait_recv()

        for slot in range(base):
            arrive(slot)
        if extra:
            pl.when(extra_of(other) < extra)(lambda: arrive(base))

    def line_copy(src, way):
        return pltpu.make_async_remote_copy(
            src_ref=abuf.at[src], dst_ref=abuf.at[src],
            send_sem=gs.at[(way + 1) // 2, src], recv_sem=gr.at[src],
            device_id={"rep": (z + way + reps) % reps}, device_id_type=MESH,
        )

    @pl.when(z + 1 < reps)
    def _():
        line_copy(z, 1).start()

    @pl.when(z > 0)
    def _():
        line_copy(z, -1).start()

    for head in range(heads):
        for k in range(1, halves):
            w_far(k, head).wait_recv()
            w_mate(k, head).start()
    for head in range(heads):
        for k in range(halves):
            w_mate(k, head).wait_recv()
        w_local(head).wait()

    def product(src):
        return jnp.dot(abuf[src], wbuf[src], preferred_element_type=jnp.float32)

    acc[...] = product(z)
    for d in range(1, reps):
        @pl.when(z - d >= 0)
        def _():
            src = (z - d + reps) % reps
            line_copy(src, 1).wait_recv()

            @pl.when(z + 1 < reps)
            def _():
                line_copy(src, 1).start()

        @pl.when(z + d < reps)
        def _():
            src = (z + d) % reps
            line_copy(src, -1).wait_recv()

            @pl.when(z > 0)
            def _():
                line_copy(src, -1).start()

        @pl.when(z - d >= 0)
        def _():
            acc[...] += product((z - d + reps) % reps)

        @pl.when(z + d < reps)
        def _():
            acc[...] += product((z + d) % reps)

    out_ref[...] = (gate_ref[...] * acc[...]).astype(out_ref.dtype)

    for d in range(1, reps):
        dst = (z + d) % reps
        mask_copy(dst, z).wait_send()
        for kind in range(3):
            for slot in range(base):
                z_copy(kind, slot, slot * reps + dst, dst, z).wait_send()
    for n in range(extra):
        dst = (extra_rep(g, reps) + n) % reps

        @pl.when(dst != z)
        def _():
            for kind in range(3):
                z_copy(kind, base, base * reps + n, dst, z).wait_send()

    def sent(slot):
        for kind in range(2):
            for rep in range(reps):
                for d in range(1, frames):
                    x_copy(kind, slot, rep, d).wait_send()
        for d in range(1, groups):
            att_copy(slot, (g + d) % groups).wait_send()

    each_slot(sent)
    for head in range(heads):
        for k in range(1, halves):
            w_far(k, head).wait_send()
        for k in range(halves):
            w_mate(k, head).wait_send()

    @pl.when(z + 1 < reps)
    def _():
        for src in range(reps):
            pl.when(src <= z)(lambda: line_copy(src, 1).wait_send())

    @pl.when(z > 0)
    def _():
        for src in range(reps):
            pl.when(src >= z)(lambda: line_copy(src, -1).wait_send())


def shards(queries, keys, values, block_lists, list_counts, out_weight, gate):
    frames, groups, reps = (lax.axis_size(a) for a in ("tm", "heads", "rep"))
    toks = queries.shape[0]
    heads = queries.shape[1] // HD
    wide = out_weight.shape[1]
    base, extra = heads // reps, heads % reps
    slots = base + (1 if extra else 0)
    assert groups == reps and groups % 2 == 0
    plane_heads = heads * groups // reps
    span = reps * toks
    lanes = -(-(span * frames // BLOCK) // 128) * 128
    dims = (frames, groups, reps, toks, heads, base, extra, slots, plane_heads)
    others = max(frames - 1, 1)
    halves = groups // 2
    vmem, smem, hbm = (
        pl.BlockSpec(memory_space=m) for m in (pltpu.VMEM, pltpu.SMEM, pl.ANY)
    )
    dma = pltpu.SemaphoreType.DMA
    scores = slots * span * span * frames
    return pl.pallas_call(
        functools.partial(kernel, dims),
        out_shape=jax.ShapeDtypeStruct((toks, wide), jnp.bfloat16),
        in_specs=[hbm, hbm, hbm, smem, smem, hbm, vmem],
        out_specs=vmem,
        scratch_shapes=[
            pltpu.VMEM((slots, span, HD), jnp.bfloat16),
            pltpu.VMEM((slots, frames, span, HD), jnp.bfloat16),
            pltpu.VMEM((slots, frames, span, HD), jnp.bfloat16),
            pltpu.VMEM((reps, 8, lanes), jnp.float32),
            pltpu.VMEM((slots, span, HD), jnp.bfloat16),
            pltpu.VMEM((reps, toks, plane_heads * HD), jnp.bfloat16),
            pltpu.VMEM((reps, plane_heads * HD, wide), jnp.bfloat16),
            pltpu.VMEM((toks, wide), jnp.float32),
            dma((3, slots, reps)), dma((3, slots, reps)),
            dma((reps,)), dma((reps,)),
            dma((2, slots, reps, others)), dma((2, slots, reps, others)),
            dma((3, slots)), dma((heads,)),
            dma((slots, groups)), dma((slots, groups)),
            dma((2, reps)), dma((reps,)),
            dma((max(halves - 1, 1), heads)), dma((max(halves - 1, 1), heads)),
            dma((halves, heads)), dma((halves, heads)),
        ],
        compiler_params=pltpu.CompilerParams(
            collective_id=0, has_side_effects=True, vmem_limit_bytes=56 * 2**20
        ),
        cost_estimate=pl.CostEstimate(
            flops=4 * scores * HD + 2 * toks * plane_heads * HD * reps * wide,
            bytes_accessed=2 * (3 * queries.size + out_weight.size),
            transcendentals=scores,
        ),
    )(queries, keys, values, block_lists, list_counts, out_weight, gate.reshape(1, wide))


def solution(mesh):
    placed = (
        P(("tm", "rep"), "heads"),
        P(("tm", "rep"), "heads"),
        P(("tm", "rep"), "heads"),
        P(("tm", "rep"), None),
        P(("tm", "rep")),
        P("heads", "rep"),
        P("rep"),
    )
    return jax.shard_map(
        shards, mesh=mesh, in_specs=placed, out_specs=P(("tm", "heads"), "rep"), check_vma=False
    )
```

```python
import functools

import jax
import jax.numpy as jnp
from jax import lax
from jax.experimental import pallas as pl
from jax.experimental.pallas import tpu as pltpu
from jax.sharding import PartitionSpec as P

HD = 128
BLOCK = 128
LIST = 16
NEG = 1e30
MESH = pl.DeviceIdType.MESH


def extra_rep(g, reps):
    half = g // 2
    return ((1 - g % 2) * half + (g % 2) * (reps - 1 - half)) % reps


def kernel(
    dims,
    q_ref, k_ref, v_ref, lists_ref, counts_ref, w_ref,
    out_ref,
    qbuf, kbuf, vbuf, mbuf, bias_buf, stage, abuf, wbuf,
    zs, zr, zms, zmr, xs, xr, own_sem, w_own, ats, atr, gs, gr, wys, wyr, wxs, wxr, wms, wmr,
):
    frames, groups, reps, toks, heads, base, extra, parts = dims
    tm = lax.axis_index("tm")
    g = lax.axis_index("heads")
    z = lax.axis_index("rep")
    span = reps * toks
    local_blocks = toks // BLOCK
    frame_blocks = span // BLOCK
    lanes = mbuf.shape[-1]
    part_cols = w_ref.shape[1] // parts
    halves = groups // 2

    def cols(head):
        return pl.ds(pl.multiple_of(head * HD, HD), HD)

    def rows(rep):
        return pl.ds(pl.multiple_of(rep * toks, toks), toks)

    def extra_rank(plane, group):
        return sum(
            jnp.where((other < group) & ((plane - extra_rep(other, reps) + reps) % reps < extra), 1, 0)
            for other in range(groups)
        )

    def extra_of(group):
        return (z - extra_rep(group, reps) + reps) % reps

    my_extra = extra_of(g)
    has_extra = my_extra < extra

    def place(group, head):
        if head < base * reps:
            return head % reps, (head // reps) * groups + group
        plane = (extra_rep(group, reps) + head - base * reps) % reps
        return plane, base * groups + extra_rank(plane, group)

    barrier = pltpu.get_barrier_semaphore()
    for axis, count, me in (("rep", reps, z), ("tm", frames, tm), ("heads", groups, g)):
        for d in range(1, count):
            pl.semaphore_signal(
                barrier, inc=1, device_id={axis: (me + d) % count}, device_id_type=MESH
            )
    pl.semaphore_wait(barrier, reps + frames + groups - 3)

    def mask_copy(dst, src):
        return pltpu.make_async_remote_copy(
            src_ref=mbuf.at[src], dst_ref=mbuf.at[src],
            send_sem=zms.at[dst], recv_sem=zmr.at[src],
            device_id={"rep": dst}, device_id_type=MESH,
        )

    sources = (k_ref, v_ref, q_ref)

    def landing(kind, slot, rep):
        if kind == 2:
            return qbuf.at[slot, rows(rep)]
        return (kbuf, vbuf)[kind].at[slot, tm, rows(rep)]

    def z_copy(kind, slot, head, dst, src):
        return pltpu.make_async_remote_copy(
            src_ref=sources[kind].at[:, cols(head)], dst_ref=landing(kind, slot, src),
            send_sem=zs.at[kind, slot, dst], recv_sem=zr.at[kind, slot, src],
            device_id={"rep": dst}, device_id_type=MESH,
        )

    def own_copy(kind, slot, head):
        return pltpu.make_async_copy(
            sources[kind].at[:, cols(head)], landing(kind, slot, z), own_sem.at[kind, slot]
        )

    def x_copy(kind, slot, rep, d, src=None):
        there = landing(kind, slot, rep)
        return pltpu.make_async_remote_copy(
            src_ref=there if src is None else src, dst_ref=there,
            send_sem=xs.at[kind, slot, rep, d - 1], recv_sem=xr.at[kind, slot, rep, d - 1],
            device_id={"tm": (tm + d) % frames}, device_id_type=MESH,
        )

    def my_head(slot):
        return slot * reps + z if slot < base else base * reps + my_extra

    def if_extra(act):
        if extra:
            pl.when(has_extra)(lambda: act(base))

    def each_base(act):
        for slot in range(base):
            act(slot)

    def start_own(kind, slot):
        if kind < 2:
            for d in range(1, frames):
                x_copy(kind, slot, z, d, sources[kind].at[:, cols(my_head(slot))]).start()
        own_copy(kind, slot, my_head(slot)).start()

    for kind in range(3):
        for d in range(1, reps):
            dst = (z + d) % reps
            each_base(lambda slot: z_copy(kind, slot, slot * reps + dst, dst, z).start())
        each_base(lambda slot: start_own(kind, slot))

    mate = g + 1 - 2 * (g % 2)
    pieces = heads * parts

    def w_here(piece):
        return w_ref.at[
            pl.ds(piece // parts * HD, HD), pl.ds(piece % parts * part_cols, part_cols)
        ]

    def w_there(group, piece):
        plane, at = place(group, piece // parts)
        return wbuf.at[plane, cols(at), pl.ds(piece % parts * part_cols, part_cols)]

    def w_far(k, piece):
        return pltpu.make_async_remote_copy(
            src_ref=w_here(piece), dst_ref=w_there(g, piece),
            send_sem=wys.at[k - 1, piece], recv_sem=wyr.at[k - 1, piece],
            device_id={"heads": (g + 2 * k) % groups}, device_id_type=MESH,
        )

    def w_frame(k, piece, d):
        there = w_there((g - 2 * k + groups) % groups, piece)
        return pltpu.make_async_remote_copy(
            src_ref=there, dst_ref=there,
            send_sem=wxs.at[k - 1, piece, d - 1], recv_sem=wxr.at[k - 1, piece],
            device_id={"tm": (tm + d) % frames}, device_id_type=MESH,
        )

    def w_mate(k, piece):
        there = w_there((g - 2 * k + groups) % groups, piece)
        return pltpu.make_async_remote_copy(
            src_ref=there if k else w_here(piece), dst_ref=there,
            send_sem=wms.at[k, piece], recv_sem=wmr.at[k, piece],
            device_id={"heads": mate}, device_id_type=MESH,
        )

    def w_local(piece):
        return pltpu.make_async_copy(w_here(piece), w_there(g, piece), w_own.at[piece])

    def w_share(act, mine=True):
        for piece in range(pieces):
            fetch = tm == piece % frames

            @pl.when(fetch if mine else jnp.logical_not(fetch))
            def _():
                for k in range(1, halves):
                    act(k, piece)

    w_share(lambda k, piece: w_far(k, piece).start())

    row_id = lax.broadcasted_iota(jnp.int32, (8, lanes), 0)
    lane_id = lax.broadcasted_iota(jnp.int32, (8, lanes), 1)
    allowed = jnp.zeros((8, lanes), jnp.float32)
    for b in range(local_blocks):
        used = counts_ref[b]
        for j in range(LIST):
            hit = (lane_id == lists_ref[b, j]) & (row_id == b) & (jnp.full((8, lanes), j) < used)
            allowed = jnp.where(hit, 1.0, allowed)
    mbuf[z] = allowed
    for d in range(1, reps):
        mask_copy((z + d) % reps, z).start()

    for kind in range(3):
        for n in range(extra):
            dst = (extra_rep(g, reps) + n) % reps

            @pl.when(dst != z)
            def _():
                z_copy(kind, base, base * reps + n, dst, z).start()

        if_extra(lambda slot: start_own(kind, slot))

    for piece in range(pieces):
        w_mate(0, piece).start()
        w_local(piece).start()

    for d in range(1, reps):
        mask_copy(z, (z + d) % reps).wait_recv()
    mask_rows = mbuf[...].reshape(reps * 8, lanes).astype(jnp.bfloat16)
    block_of = lax.broadcasted_iota(jnp.int32, (lanes, span), 1) // BLOCK
    lane_of = lax.broadcasted_iota(jnp.int32, (lanes, span), 0)

    def spread_mask(frame, _):
        spread = jnp.where(block_of + frame * frame_blocks == lane_of, 1.0, 0.0)
        hits = jnp.dot(
            mask_rows, spread.astype(jnp.bfloat16), preferred_element_type=jnp.float32
        )
        bias_buf[frame] = (NEG * (hits - 1.0)).reshape(reps, 8, span)
        return 0

    lax.fori_loop(0, frames, spread_mask, 0)

    def pass_on(slot):
        for kind in range(2):
            for d in range(1, reps):
                src = (z + d) % reps
                z_copy(kind, slot, 0, z, src).wait_recv()
                for e in range(1, frames):
                    x_copy(kind, slot, src, e).start()

    def rest(slot):
        for kind in range(3):
            own_copy(kind, slot, my_head(slot)).wait()
        for kind in range(2):
            for rep in range(reps):
                for d in range(1, frames):
                    there = (kbuf, vbuf)[kind].at[slot, (tm - d + frames) % frames, rows(rep)]
                    pltpu.make_async_remote_copy(
                        src_ref=there, dst_ref=there,
                        send_sem=xs.at[kind, slot, rep, d - 1],
                        recv_sem=xr.at[kind, slot, rep, d - 1],
                        device_id={"tm": (tm + d) % frames}, device_id_type=MESH,
                    ).wait_recv()

    def attend(slot, chunk):
        queries = qbuf[slot, rows(chunk)]
        factor = 1.4426950408889634 / HD**0.5

        def step(frame, state):
            top, total, sums = state
            bias = bias_buf[frame, chunk]
            scores = lax.dot_general(
                queries, kbuf[slot, frame], (((1,), (1,)), ((), ())),
                preferred_element_type=jnp.float32,
            )
            scores = scores + jnp.concatenate(
                [jnp.broadcast_to(bias[b : b + 1], (BLOCK, span)) for b in range(local_blocks)], 0
            )
            new_top = jnp.maximum(top, jnp.max(scores, axis=1, keepdims=True))
            weights = jnp.exp2((scores - new_top) * factor)
            scale = jnp.exp2((top - new_top) * factor)
            total = total * scale + jnp.sum(weights, axis=1, keepdims=True)
            sums = sums * scale + jnp.dot(
                weights.astype(jnp.bfloat16), vbuf[slot, frame], preferred_element_type=jnp.float32
            )
            return new_top, total, sums

        state = (
            jnp.full((toks, 1), -NEG, jnp.float32),
            jnp.zeros((toks, 1), jnp.float32),
            jnp.zeros((toks, HD), jnp.float32),
        )
        _, total, sums = lax.fori_loop(0, frames, step, state, unroll=min(frames, 2))
        stage[slot, rows(chunk)] = (sums / total).astype(jnp.bfloat16)

    def position(slot, group):
        return slot * groups + group if slot < base else base * groups + extra_rank(z, group)

    def att_copy(slot, chunk):
        return pltpu.make_async_remote_copy(
            src_ref=stage.at[slot, rows(chunk)], dst_ref=abuf.at[z, :, cols(position(slot, g))],
            send_sem=ats.at[slot, chunk], recv_sem=atr.at[slot, g],
            device_id={"heads": chunk}, device_id_type=MESH,
        )

    def att_local(slot):
        return pltpu.make_async_copy(
            stage.at[slot, rows(g)], abuf.at[z, :, cols(position(slot, g))], ats.at[slot, g]
        )

    def arrive(slot, other):
        there = abuf.at[z, :, cols(position(slot, other))]
        pltpu.make_async_remote_copy(
            src_ref=stage.at[slot, rows(g)], dst_ref=there,
            send_sem=ats.at[slot, other], recv_sem=atr.at[slot, other],
            device_id={"heads": other}, device_id_type=MESH,
        ).wait_recv()

    def attend_all(slot):
        def one_chunk(i, _):
            chunk = (z + i) % reps

            @pl.when(i > 0)
            def _():
                z_copy(2, slot, 0, z, chunk).wait_recv()

            attend(slot, chunk)

            @pl.when(chunk != g)
            def _():
                att_copy(slot, chunk).start()

            @pl.when(chunk == g)
            def _():
                att_local(slot).start()

            return 0

        lax.fori_loop(0, reps, one_chunk, 0)

    line_cols = (pl.ds(0, base * groups * HD), pl.ds(base * groups * HD, (heads - base * reps) * HD))
    line_parts = 2 if extra else 1

    def line_copy(part, src, way):
        there = abuf.at[src, :, line_cols[part]]
        return pltpu.make_async_remote_copy(
            src_ref=there, dst_ref=there,
            send_sem=gs.at[part, (way + 1) // 2, src], recv_sem=gr.at[part, src],
            device_id={"rep": (z + way + reps) % reps}, device_id_type=MESH,
        )

    def line_start(part):
        @pl.when(z + 1 < reps)
        def _():
            line_copy(part, z, 1).start()

        @pl.when(z > 0)
        def _():
            line_copy(part, z, -1).start()

    def line_relay(part, d):
        @pl.when(z - d >= 0)
        def _():
            src = (z - d + reps) % reps
            line_copy(part, src, 1).wait_recv()

            @pl.when(z + 1 < reps)
            def _():
                line_copy(part, src, 1).start()

        @pl.when(z + d < reps)
        def _():
            src = (z + d) % reps
            line_copy(part, src, -1).wait_recv()

            @pl.when(z > 0)
            def _():
                line_copy(part, src, -1).start()

    each_base(pass_on)
    each_base(rest)
    each_base(attend_all)
    if_extra(pass_on)

    def send_on(k, piece):
        w_far(k, piece).wait_recv()
        for d in range(1, frames):
            w_frame(k, piece, d).start()
        w_mate(k, piece).start()

    w_share(send_on)
    each_base(lambda slot: att_local(slot).wait())
    for d in range(1, groups):
        each_base(lambda slot: arrive(slot, (g + d) % groups))
    line_start(0)

    if_extra(rest)
    if_extra(attend_all)
    for d in range(1, reps - 1):
        line_relay(0, d)
        if d == 1 and extra:
            if_extra(lambda slot: att_local(slot).wait())
            for e in range(1, groups):
                other = (g + e) % groups
                pl.when(extra_of(other) < extra)(lambda: arrive(base, other))
            line_start(1)
    if extra:
        for d in range(1, reps - 1):
            line_relay(1, d)

    def to_mate(k, piece):
        w_frame(k, piece, 1).wait_recv()
        w_mate(k, piece).start()

    w_share(to_mate, mine=False)
    for piece in range(pieces):
        for k in range(halves):
            w_mate(k, piece).wait_recv()
        w_local(piece).wait()

    def product(src):
        return jnp.dot(abuf[src], wbuf[src], preferred_element_type=jnp.float32)

    out_ref[...] = product(z)
    for d in range(1, reps):
        if d == reps - 1:
            for part in range(line_parts):
                line_relay(part, d)

        @pl.when(z - d >= 0)
        def _():
            out_ref[...] += product((z - d + reps) % reps)

        @pl.when(z + d < reps)
        def _():
            out_ref[...] += product((z + d) % reps)

    for d in range(1, reps):
        dst = (z + d) % reps
        mask_copy(dst, z).wait_send()
        for kind in range(3):
            each_base(lambda slot: z_copy(kind, slot, slot * reps + dst, dst, z).wait_send())
    for n in range(extra):
        dst = (extra_rep(g, reps) + n) % reps

        @pl.when(dst != z)
        def _():
            for kind in range(3):
                z_copy(kind, base, base * reps + n, dst, z).wait_send()

    def sent(slot):
        for kind in range(2):
            for rep in range(reps):
                for d in range(1, frames):
                    x_copy(kind, slot, rep, d).wait_send()
        for d in range(1, groups):
            att_copy(slot, (g + d) % groups).wait_send()

    each_base(sent)
    if_extra(sent)

    def share_sent(k, piece):
        w_far(k, piece).wait_send()
        for d in range(1, frames):
            w_frame(k, piece, d).wait_send()

    w_share(share_sent)
    for piece in range(pieces):
        for k in range(halves):
            w_mate(k, piece).wait_send()

    for part in range(line_parts):
        @pl.when(z + 1 < reps)
        def _():
            for src in range(reps):
                pl.when(src <= z)(lambda: line_copy(part, src, 1).wait_send())

        @pl.when(z > 0)
        def _():
            for src in range(reps):
                pl.when(src >= z)(lambda: line_copy(part, src, -1).wait_send())


def shards(queries, keys, values, block_lists, list_counts, out_weight, gate):
    frames, groups, reps = (lax.axis_size(a) for a in ("tm", "heads", "rep"))
    toks = queries.shape[0]
    heads = queries.shape[1] // HD
    wide = out_weight.shape[1]
    base, extra = heads // reps, heads % reps
    slots = base + (1 if extra else 0)
    assert groups == reps and groups % 2 == 0
    plane_heads = heads * groups // reps
    span = reps * toks
    lanes = -(-(span * frames // BLOCK) // 128) * 128
    parts = 2 if wide % 256 == 0 else 1
    dims = (frames, groups, reps, toks, heads, base, extra, parts)
    others = max(frames - 1, 1)
    halves = groups // 2
    far = max(halves - 1, 1)
    pieces = heads * parts
    vmem, smem, hbm = (
        pl.BlockSpec(memory_space=m) for m in (pltpu.VMEM, pltpu.SMEM, pl.ANY)
    )
    dma = pltpu.SemaphoreType.DMA
    scores = slots * span * span * frames
    summed = pl.pallas_call(
        functools.partial(kernel, dims),
        out_shape=jax.ShapeDtypeStruct((toks, wide), jnp.float32),
        in_specs=[hbm, hbm, hbm, smem, smem, hbm],
        out_specs=vmem,
        scratch_shapes=[
            pltpu.VMEM((slots, span, HD), jnp.bfloat16),
            pltpu.VMEM((slots, frames, span, HD), jnp.bfloat16),
            pltpu.VMEM((slots, frames, span, HD), jnp.bfloat16),
            pltpu.VMEM((reps, 8, lanes), jnp.float32),
            pltpu.VMEM((frames, reps, 8, span), jnp.float32),
            pltpu.VMEM((slots, span, HD), jnp.bfloat16),
            pltpu.VMEM((reps, toks, plane_heads * HD), jnp.bfloat16),
            pltpu.VMEM((reps, plane_heads * HD, wide), jnp.bfloat16),
            dma((3, slots, reps)), dma((3, slots, reps)),
            dma((reps,)), dma((reps,)),
            dma((2, slots, reps, others)), dma((2, slots, reps, others)),
            dma((3, slots)), dma((pieces,)),
            dma((slots, groups)), dma((slots, groups)),
            dma((2, 2, reps)), dma((2, reps)),
            dma((far, pieces)), dma((far, pieces)),
            dma((far, pieces, others)), dma((far, pieces)),
            dma((halves, pieces)), dma((halves, pieces)),
        ],
        compiler_params=pltpu.CompilerParams(
            collective_id=0, has_side_effects=True, vmem_limit_bytes=56 * 2**20
        ),
        cost_estimate=pl.CostEstimate(
            flops=4 * scores * HD + 2 * toks * plane_heads * HD * reps * wide,
            bytes_accessed=2 * (3 * queries.size + out_weight.size),
            transcendentals=scores,
        ),
    )(queries, keys, values, block_lists, list_counts, out_weight)
    return (gate[None, :] * summed).astype(jnp.bfloat16)


def solution(mesh):
    placed = (
        P(("tm", "rep"), "heads"),
        P(("tm", "rep"), "heads"),
        P(("tm", "rep"), "heads"),
        P(("tm", "rep"), None),
        P(("tm", "rep")),
        P("heads", "rep"),
        P("rep"),
    )
    return jax.shard_map(
        shards, mesh=mesh, in_specs=placed, out_specs=P(("tm", "heads"), "rep"), check_vma=False
    )
```

```python
import functools

import jax
import jax.numpy as jnp
from jax import lax
from jax.experimental import pallas as pl
from jax.experimental.pallas import tpu as pltpu
from jax.sharding import PartitionSpec as P

HD = 128
BLOCK = 128
LIST = 16
NEG = 1e30
MESH = pl.DeviceIdType.MESH


def extra_rep(g, reps):
    half = g // 2
    return ((1 - g % 2) * half + (g % 2) * (reps - 1 - half)) % reps


def kernel(
    dims,
    q_ref, k_ref, v_ref, lists_ref, counts_ref, w_ref,
    out_ref,
    qbuf, kbuf, vbuf, mbuf, bias_buf, stage, abuf, wbuf,
    zs, zr, zms, zmr, xs, xr, own_sem, w_own, ats, atr, gs, gr, wys, wyr, wxs, wxr, wms, wmr,
):
    frames, groups, reps, toks, heads, base, extra, parts = dims
    tm = lax.axis_index("tm")
    g = lax.axis_index("heads")
    z = lax.axis_index("rep")
    span = reps * toks
    local_blocks = toks // BLOCK
    frame_blocks = span // BLOCK
    lanes = mbuf.shape[-1]
    part_cols = w_ref.shape[1] // parts
    halves = groups // 2

    def cols(head):
        return pl.ds(pl.multiple_of(head * HD, HD), HD)

    def rows(rep):
        return pl.ds(pl.multiple_of(rep * toks, toks), toks)

    def extra_rank(plane, group):
        return sum(
            jnp.where((other < group) & ((plane - extra_rep(other, reps) + reps) % reps < extra), 1, 0)
            for other in range(groups)
        )

    def extra_of(group):
        return (z - extra_rep(group, reps) + reps) % reps

    my_extra = extra_of(g)
    has_extra = my_extra < extra

    def place(group, head):
        if head < base * reps:
            return head % reps, (head // reps) * groups + group
        plane = (extra_rep(group, reps) + head - base * reps) % reps
        return plane, base * groups + extra_rank(plane, group)

    barrier = pltpu.get_barrier_semaphore()
    for axis, count, me in (("rep", reps, z), ("tm", frames, tm), ("heads", groups, g)):
        for d in range(1, count):
            pl.semaphore_signal(
                barrier, inc=1, device_id={axis: (me + d) % count}, device_id_type=MESH
            )
    pl.semaphore_wait(barrier, reps + frames + groups - 3)

    def mask_copy(dst, src):
        return pltpu.make_async_remote_copy(
            src_ref=mbuf.at[src], dst_ref=mbuf.at[src],
            send_sem=zms.at[dst], recv_sem=zmr.at[src],
            device_id={"rep": dst}, device_id_type=MESH,
        )

    sources = (k_ref, v_ref, q_ref)

    def landing(kind, slot, rep):
        if kind == 2:
            return qbuf.at[slot, rows(rep)]
        return (kbuf, vbuf)[kind].at[slot, tm, rows(rep)]

    def z_copy(kind, slot, head, dst, src):
        return pltpu.make_async_remote_copy(
            src_ref=sources[kind].at[:, cols(head)], dst_ref=landing(kind, slot, src),
            send_sem=zs.at[kind, slot, dst], recv_sem=zr.at[kind, slot, src],
            device_id={"rep": dst}, device_id_type=MESH,
        )

    def own_copy(kind, slot, head):
        return pltpu.make_async_copy(
            sources[kind].at[:, cols(head)], landing(kind, slot, z), own_sem.at[kind, slot]
        )

    def x_copy(kind, slot, rep, d, src=None):
        there = landing(kind, slot, rep)
        return pltpu.make_async_remote_copy(
            src_ref=there if src is None else src, dst_ref=there,
            send_sem=xs.at[kind, slot, rep, d - 1], recv_sem=xr.at[kind, slot, rep, d - 1],
            device_id={"tm": (tm + d) % frames}, device_id_type=MESH,
        )

    def my_head(slot):
        return slot * reps + z if slot < base else base * reps + my_extra

    def if_extra(act):
        if extra:
            pl.when(has_extra)(lambda: act(base))

    def each_base(act):
        for slot in range(base):
            act(slot)

    def start_own(kind, slot):
        if kind < 2:
            for d in range(1, frames):
                x_copy(kind, slot, z, d, sources[kind].at[:, cols(my_head(slot))]).start()
        own_copy(kind, slot, my_head(slot)).start()

    def wave(kind, d, act):
        dst = (z + d) % reps
        each_base(lambda slot: act(z_copy(kind, slot, slot * reps + dst, dst, z)))
        for n in range(extra):
            pl.when((extra_rep(g, reps) + n) % reps == dst)(
                lambda: act(z_copy(kind, base, base * reps + n, dst, z))
            )

    for d in range(1, reps):
        wave(0, d, lambda copy: copy.start())
    for kind in range(3):
        each_base(lambda slot: start_own(kind, slot))

    mate = g + 1 - 2 * (g % 2)
    pieces = heads * parts

    def w_here(piece):
        return w_ref.at[
            pl.ds(piece // parts * HD, HD), pl.ds(piece % parts * part_cols, part_cols)
        ]

    def w_there(group, piece):
        plane, at = place(group, piece // parts)
        return wbuf.at[plane, cols(at), pl.ds(piece % parts * part_cols, part_cols)]

    def w_far(k, piece):
        return pltpu.make_async_remote_copy(
            src_ref=w_here(piece), dst_ref=w_there(g, piece),
            send_sem=wys.at[k - 1, piece], recv_sem=wyr.at[k - 1, piece],
            device_id={"heads": (g + 2 * k) % groups}, device_id_type=MESH,
        )

    def w_frame(k, piece, d):
        there = w_there((g - 2 * k + groups) % groups, piece)
        return pltpu.make_async_remote_copy(
            src_ref=there, dst_ref=there,
            send_sem=wxs.at[k - 1, piece, d - 1], recv_sem=wxr.at[k - 1, piece],
            device_id={"tm": (tm + d) % frames}, device_id_type=MESH,
        )

    def w_mate(k, piece):
        there = w_there((g - 2 * k + groups) % groups, piece)
        return pltpu.make_async_remote_copy(
            src_ref=there if k else w_here(piece), dst_ref=there,
            send_sem=wms.at[k, piece], recv_sem=wmr.at[k, piece],
            device_id={"heads": mate}, device_id_type=MESH,
        )

    def w_local(piece):
        return pltpu.make_async_copy(w_here(piece), w_there(g, piece), w_own.at[piece])

    def w_share(act, mine=True):
        for piece in range(pieces):
            fetch = tm == piece % frames

            @pl.when(fetch if mine else jnp.logical_not(fetch))
            def _():
                for k in range(1, halves):
                    act(k, piece)

    w_share(lambda k, piece: w_far(k, piece).start())

    row_id = lax.broadcasted_iota(jnp.int32, (8, lanes), 0)
    lane_id = lax.broadcasted_iota(jnp.int32, (8, lanes), 1)
    allowed = jnp.zeros((8, lanes), jnp.float32)
    for b in range(local_blocks):
        used = counts_ref[b]
        for j in range(LIST):
            hit = (lane_id == lists_ref[b, j]) & (row_id == b) & (jnp.full((8, lanes), j) < used)
            allowed = jnp.where(hit, 1.0, allowed)
    mbuf[z] = allowed
    for d in range(1, reps):
        mask_copy((z + d) % reps, z).start()

    for kind in range(3):
        if_extra(lambda slot: start_own(kind, slot))

    for piece in range(pieces):
        w_mate(0, piece).start()
        w_local(piece).start()

    for d in range(1, reps):
        mask_copy(z, (z + d) % reps).wait_recv()
    mask_rows = mbuf[...].reshape(reps * 8, lanes).astype(jnp.bfloat16)
    block_of = lax.broadcasted_iota(jnp.int32, (lanes, span), 1) // BLOCK
    lane_of = lax.broadcasted_iota(jnp.int32, (lanes, span), 0)

    def spread_mask(frame, _):
        spread = jnp.where(block_of + frame * frame_blocks == lane_of, 1.0, 0.0)
        hits = jnp.dot(
            mask_rows, spread.astype(jnp.bfloat16), preferred_element_type=jnp.float32
        )
        bias_buf[frame] = (NEG * (hits - 1.0)).reshape(reps, 8, span)
        return 0

    lax.fori_loop(0, frames, spread_mask, 0)

    def pass_on(kind, src, slot):
        z_copy(kind, slot, 0, z, src).wait_recv()
        for e in range(1, frames):
            x_copy(kind, slot, src, e).start()

    def rest(slot):
        for kind in range(3):
            own_copy(kind, slot, my_head(slot)).wait()
        for kind in range(2):
            for rep in range(reps):
                for d in range(1, frames):
                    there = (kbuf, vbuf)[kind].at[slot, (tm - d + frames) % frames, rows(rep)]
                    pltpu.make_async_remote_copy(
                        src_ref=there, dst_ref=there,
                        send_sem=xs.at[kind, slot, rep, d - 1],
                        recv_sem=xr.at[kind, slot, rep, d - 1],
                        device_id={"tm": (tm + d) % frames}, device_id_type=MESH,
                    ).wait_recv()

    def attend(slot, chunk):
        queries = qbuf[slot, rows(chunk)]
        factor = 1.4426950408889634 / HD**0.5

        def step(frame, state):
            top, total, sums = state
            bias = bias_buf[frame, chunk]
            scores = lax.dot_general(
                queries, kbuf[slot, frame], (((1,), (1,)), ((), ())),
                preferred_element_type=jnp.float32,
            )
            scores = scores + jnp.concatenate(
                [jnp.broadcast_to(bias[b : b + 1], (BLOCK, span)) for b in range(local_blocks)], 0
            )
            new_top = jnp.maximum(top, jnp.max(scores, axis=1, keepdims=True))
            weights = jnp.exp2((scores - new_top) * factor)
            scale = jnp.exp2((top - new_top) * factor)
            total = total * scale + jnp.sum(weights, axis=1, keepdims=True)
            sums = sums * scale + jnp.dot(
                weights.astype(jnp.bfloat16), vbuf[slot, frame], preferred_element_type=jnp.float32
            )
            return new_top, total, sums

        state = (
            jnp.full((toks, 1), -NEG, jnp.float32),
            jnp.zeros((toks, 1), jnp.float32),
            jnp.zeros((toks, HD), jnp.float32),
        )
        _, total, sums = lax.fori_loop(0, frames, step, state, unroll=min(frames, 2))
        stage[slot, rows(chunk)] = (sums / total).astype(jnp.bfloat16)

    def position(slot, group):
        return slot * groups + group if slot < base else base * groups + extra_rank(z, group)

    def att_copy(slot, chunk):
        return pltpu.make_async_remote_copy(
            src_ref=stage.at[slot, rows(chunk)], dst_ref=abuf.at[z, :, cols(position(slot, g))],
            send_sem=ats.at[slot, chunk], recv_sem=atr.at[slot, g],
            device_id={"heads": chunk}, device_id_type=MESH,
        )

    def att_local(slot):
        return pltpu.make_async_copy(
            stage.at[slot, rows(g)], abuf.at[z, :, cols(position(slot, g))], ats.at[slot, g]
        )

    def arrive(slot, other):
        there = abuf.at[z, :, cols(position(slot, other))]
        pltpu.make_async_remote_copy(
            src_ref=stage.at[slot, rows(g)], dst_ref=there,
            send_sem=ats.at[slot, other], recv_sem=atr.at[slot, other],
            device_id={"heads": other}, device_id_type=MESH,
        ).wait_recv()

    def attend_all(slot, beside=lambda: None):
        def one_chunk(i, _):
            chunk = (z + i) % reps

            @pl.when(i > 0)
            def _():
                z_copy(2, slot, 0, z, chunk).wait_recv()

            attend(slot, chunk)
            pl.when(i == 0)(beside)

            @pl.when(chunk != g)
            def _():
                att_copy(slot, chunk).start()

            @pl.when(chunk == g)
            def _():
                att_local(slot).start()

            return 0

        lax.fori_loop(0, reps, one_chunk, 0)

    line_cols = (pl.ds(0, base * groups * HD), pl.ds(base * groups * HD, (heads - base * reps) * HD))
    line_parts = 2 if extra else 1

    def line_copy(part, src, way):
        there = abuf.at[src, :, line_cols[part]]
        return pltpu.make_async_remote_copy(
            src_ref=there, dst_ref=there,
            send_sem=gs.at[part, (way + 1) // 2, src], recv_sem=gr.at[part, src],
            device_id={"rep": (z + way + reps) % reps}, device_id_type=MESH,
        )

    def line_start(part):
        @pl.when(z + 1 < reps)
        def _():
            line_copy(part, z, 1).start()

        @pl.when(z > 0)
        def _():
            line_copy(part, z, -1).start()

    def line_relay(part, d):
        @pl.when(z - d >= 0)
        def _():
            src = (z - d + reps) % reps
            line_copy(part, src, 1).wait_recv()

            @pl.when(z + 1 < reps)
            def _():
                line_copy(part, src, 1).start()

        @pl.when(z + d < reps)
        def _():
            src = (z + d) % reps
            line_copy(part, src, -1).wait_recv()

            @pl.when(z > 0)
            def _():
                line_copy(part, src, -1).start()

    for kind in range(2):
        for d in range(1, reps):
            wave(kind, d, lambda copy: copy.wait_send())
            wave(kind + 1, d, lambda copy: copy.start())
        for d in range(1, reps):
            src = (z - d + reps) % reps
            each_base(lambda slot: pass_on(kind, src, slot))
            if_extra(lambda slot: pass_on(kind, src, slot))
    each_base(rest)

    def send_on(k, piece):
        w_far(k, piece).wait_recv()
        for d in range(1, frames):
            w_frame(k, piece, d).start()
        w_mate(k, piece).start()

    each_base(lambda slot: attend_all(slot, lambda: w_share(send_on) if slot == 0 else None))
    each_base(lambda slot: att_local(slot).wait())
    for d in range(1, groups):
        each_base(lambda slot: arrive(slot, (g + d) % groups))
    line_start(0)

    if_extra(rest)
    if_extra(attend_all)
    for d in range(1, reps - 1):
        line_relay(0, d)
        if d == 1 and extra:
            if_extra(lambda slot: att_local(slot).wait())
            for e in range(1, groups):
                other = (g + e) % groups
                pl.when(extra_of(other) < extra)(lambda: arrive(base, other))
            line_start(1)
    if extra:
        for d in range(1, reps - 1):
            line_relay(1, d)

    def to_mate(k, piece):
        w_frame(k, piece, 1).wait_recv()
        w_mate(k, piece).start()

    w_share(to_mate, mine=False)
    for piece in range(pieces):
        for k in range(halves):
            w_mate(k, piece).wait_recv()
        w_local(piece).wait()

    def product(src):
        return jnp.dot(abuf[src], wbuf[src], preferred_element_type=jnp.float32)

    out_ref[...] = product(z)
    for d in range(1, reps):
        if d == reps - 1:
            for part in range(line_parts):
                line_relay(part, d)

        @pl.when(z - d >= 0)
        def _():
            out_ref[...] += product((z - d + reps) % reps)

        @pl.when(z + d < reps)
        def _():
            out_ref[...] += product((z + d) % reps)

    for d in range(1, reps):
        mask_copy((z + d) % reps, z).wait_send()
        wave(2, d, lambda copy: copy.wait_send())

    def sent(slot):
        for kind in range(2):
            for rep in range(reps):
                for d in range(1, frames):
                    x_copy(kind, slot, rep, d).wait_send()
        for d in range(1, groups):
            att_copy(slot, (g + d) % groups).wait_send()

    each_base(sent)
    if_extra(sent)

    def share_sent(k, piece):
        w_far(k, piece).wait_send()
        for d in range(1, frames):
            w_frame(k, piece, d).wait_send()

    w_share(share_sent)
    for piece in range(pieces):
        for k in range(halves):
            w_mate(k, piece).wait_send()

    for part in range(line_parts):
        @pl.when(z + 1 < reps)
        def _():
            for src in range(reps):
                pl.when(src <= z)(lambda: line_copy(part, src, 1).wait_send())

        @pl.when(z > 0)
        def _():
            for src in range(reps):
                pl.when(src >= z)(lambda: line_copy(part, src, -1).wait_send())


def shards(queries, keys, values, block_lists, list_counts, out_weight, gate):
    frames, groups, reps = (lax.axis_size(a) for a in ("tm", "heads", "rep"))
    toks = queries.shape[0]
    heads = queries.shape[1] // HD
    wide = out_weight.shape[1]
    base, extra = heads // reps, heads % reps
    slots = base + (1 if extra else 0)
    assert groups == reps and groups % 2 == 0
    plane_heads = heads * groups // reps
    span = reps * toks
    lanes = -(-(span * frames // BLOCK) // 128) * 128
    parts = 2 if wide % 256 == 0 else 1
    dims = (frames, groups, reps, toks, heads, base, extra, parts)
    others = max(frames - 1, 1)
    halves = groups // 2
    far = max(halves - 1, 1)
    pieces = heads * parts
    vmem, smem, hbm = (
        pl.BlockSpec(memory_space=m) for m in (pltpu.VMEM, pltpu.SMEM, pl.ANY)
    )
    dma = pltpu.SemaphoreType.DMA
    scores = slots * span * span * frames
    summed = pl.pallas_call(
        functools.partial(kernel, dims),
        out_shape=jax.ShapeDtypeStruct((toks, wide), jnp.float32),
        in_specs=[hbm, hbm, hbm, smem, smem, hbm],
        out_specs=vmem,
        scratch_shapes=[
            pltpu.VMEM((slots, span, HD), jnp.bfloat16),
            pltpu.VMEM((slots, frames, span, HD), jnp.bfloat16),
            pltpu.VMEM((slots, frames, span, HD), jnp.bfloat16),
            pltpu.VMEM((reps, 8, lanes), jnp.float32),
            pltpu.VMEM((frames, reps, 8, span), jnp.float32),
            pltpu.VMEM((slots, span, HD), jnp.bfloat16),
            pltpu.VMEM((reps, toks, plane_heads * HD), jnp.bfloat16),
            pltpu.VMEM((reps, plane_heads * HD, wide), jnp.bfloat16),
            dma((3, slots, reps)), dma((3, slots, reps)),
            dma((reps,)), dma((reps,)),
            dma((2, slots, reps, others)), dma((2, slots, reps, others)),
            dma((3, slots)), dma((pieces,)),
            dma((slots, groups)), dma((slots, groups)),
            dma((2, 2, reps)), dma((2, reps)),
            dma((far, pieces)), dma((far, pieces)),
            dma((far, pieces, others)), dma((far, pieces)),
            dma((halves, pieces)), dma((halves, pieces)),
        ],
        compiler_params=pltpu.CompilerParams(
            collective_id=0, has_side_effects=True, vmem_limit_bytes=56 * 2**20
        ),
        cost_estimate=pl.CostEstimate(
            flops=4 * scores * HD + 2 * toks * plane_heads * HD * reps * wide,
            bytes_accessed=2 * (3 * queries.size + out_weight.size),
            transcendentals=scores,
        ),
    )(queries, keys, values, block_lists, list_counts, out_weight)
    return (gate[None, :] * summed).astype(jnp.bfloat16)


def solution(mesh):
    placed = (
        P(("tm", "rep"), "heads"),
        P(("tm", "rep"), "heads"),
        P(("tm", "rep"), "heads"),
        P(("tm", "rep"), None),
        P(("tm", "rep")),
        P("heads", "rep"),
        P("rep"),
    )
    return jax.shard_map(
        shards, mesh=mesh, in_specs=placed, out_specs=P(("tm", "heads"), "rep"), check_vma=False
    )
```

```python
import functools

import jax
import jax.numpy as jnp
from jax import lax
from jax.experimental import pallas as pl
from jax.experimental.pallas import tpu as pltpu
from jax.sharding import PartitionSpec as P

HD = 128
BLOCK = 128
LIST = 16
NEG = 1e30
MESH = pl.DeviceIdType.MESH


def extra_rep(g, reps):
    half = g // 2
    return ((1 - g % 2) * half + (g % 2) * (reps - 1 - half)) % reps


def kernel(
    dims,
    q_ref, k_ref, v_ref, lists_ref, counts_ref, w_ref,
    out_ref,
    qbuf, kbuf, vbuf, vturned, mbuf, stage, abuf, wbuf,
    zs, zr, zms, zmr, xs, xr, own_sem, w_own, ats, atr, gs, gr, wys, wyr, wxs, wxr, wms, wmr,
):
    frames, groups, reps, toks, heads, base, extra, parts = dims
    tm = lax.axis_index("tm")
    g = lax.axis_index("heads")
    z = lax.axis_index("rep")
    span = reps * toks
    local_blocks = toks // BLOCK
    frame_blocks = span // BLOCK
    part_cols = w_ref.shape[1] // parts
    halves = groups // 2

    def cols(head):
        return pl.ds(pl.multiple_of(head * HD, HD), HD)

    def rows(rep):
        return pl.ds(pl.multiple_of(rep * toks, toks), toks)

    def extra_rank(plane, group):
        return sum(
            jnp.where((other < group) & ((plane - extra_rep(other, reps) + reps) % reps < extra), 1, 0)
            for other in range(groups)
        )

    def extra_of(group):
        return (z - extra_rep(group, reps) + reps) % reps

    my_extra = extra_of(g)
    has_extra = my_extra < extra

    def place(group, head):
        if head < base * reps:
            return head % reps, (head // reps) * groups + group
        plane = (extra_rep(group, reps) + head - base * reps) % reps
        return plane, base * groups + extra_rank(plane, group)

    barrier = pltpu.get_barrier_semaphore()
    for axis, count, me in (("rep", reps, z), ("tm", frames, tm), ("heads", groups, g)):
        for d in range(1, count):
            pl.semaphore_signal(
                barrier, inc=1, device_id={axis: (me + d) % count}, device_id_type=MESH
            )
    pl.semaphore_wait(barrier, reps + frames + groups - 3)

    def mask_copy(dst, src):
        return pltpu.make_async_remote_copy(
            src_ref=mbuf.at[src], dst_ref=mbuf.at[src],
            send_sem=zms.at[dst], recv_sem=zmr.at[src],
            device_id={"rep": dst}, device_id_type=MESH,
        )

    sources = (k_ref, v_ref, q_ref)

    def landing(kind, slot, rep):
        if kind == 2:
            return qbuf.at[slot, rows(rep)]
        return (kbuf, vbuf)[kind].at[slot, tm, rows(rep)]

    def z_copy(kind, slot, head, dst, src):
        return pltpu.make_async_remote_copy(
            src_ref=sources[kind].at[:, cols(head)], dst_ref=landing(kind, slot, src),
            send_sem=zs.at[kind, slot, dst], recv_sem=zr.at[kind, slot, src],
            device_id={"rep": dst}, device_id_type=MESH,
        )

    def own_copy(kind, slot, head):
        return pltpu.make_async_copy(
            sources[kind].at[:, cols(head)], landing(kind, slot, z), own_sem.at[kind, slot]
        )

    def x_copy(kind, slot, rep, d, src=None):
        there = landing(kind, slot, rep)
        return pltpu.make_async_remote_copy(
            src_ref=there if src is None else src, dst_ref=there,
            send_sem=xs.at[kind, slot, rep, d - 1], recv_sem=xr.at[kind, slot, rep, d - 1],
            device_id={"tm": (tm + d) % frames}, device_id_type=MESH,
        )

    def my_head(slot):
        return slot * reps + z if slot < base else base * reps + my_extra

    def if_extra(act):
        if extra:
            pl.when(has_extra)(lambda: act(base))

    def each_base(act):
        for slot in range(base):
            act(slot)

    def start_own(kind, slot):
        if kind < 2:
            for d in range(1, frames):
                x_copy(kind, slot, z, d, sources[kind].at[:, cols(my_head(slot))]).start()
        own_copy(kind, slot, my_head(slot)).start()

    def wave(kind, d, act):
        dst = (z + d) % reps
        each_base(lambda slot: act(z_copy(kind, slot, slot * reps + dst, dst, z)))
        for n in range(extra):
            pl.when((extra_rep(g, reps) + n) % reps == dst)(
                lambda: act(z_copy(kind, base, base * reps + n, dst, z))
            )

    for d in range(1, reps):
        wave(0, d, lambda copy: copy.start())
    for kind in range(3):
        each_base(lambda slot: start_own(kind, slot))

    mate = g + 1 - 2 * (g % 2)
    pieces = heads * parts

    def w_here(piece):
        return w_ref.at[
            pl.ds(piece // parts * HD, HD), pl.ds(piece % parts * part_cols, part_cols)
        ]

    def w_there(group, piece):
        plane, at = place(group, piece // parts)
        return wbuf.at[plane, cols(at), pl.ds(piece % parts * part_cols, part_cols)]

    def w_far(k, piece):
        return pltpu.make_async_remote_copy(
            src_ref=w_here(piece), dst_ref=w_there(g, piece),
            send_sem=wys.at[k - 1, piece], recv_sem=wyr.at[k - 1, piece],
            device_id={"heads": (g + 2 * k) % groups}, device_id_type=MESH,
        )

    def w_frame(k, piece, d):
        there = w_there((g - 2 * k + groups) % groups, piece)
        return pltpu.make_async_remote_copy(
            src_ref=there, dst_ref=there,
            send_sem=wxs.at[k - 1, piece, d - 1], recv_sem=wxr.at[k - 1, piece],
            device_id={"tm": (tm + d) % frames}, device_id_type=MESH,
        )

    def w_mate(k, piece):
        there = w_there((g - 2 * k + groups) % groups, piece)
        return pltpu.make_async_remote_copy(
            src_ref=there if k else w_here(piece), dst_ref=there,
            send_sem=wms.at[k, piece], recv_sem=wmr.at[k, piece],
            device_id={"heads": mate}, device_id_type=MESH,
        )

    def w_local(piece):
        return pltpu.make_async_copy(w_here(piece), w_there(g, piece), w_own.at[piece])

    def w_share(act, mine=True):
        for piece in range(pieces):
            fetch = tm == piece % frames

            @pl.when(fetch if mine else jnp.logical_not(fetch))
            def _():
                for k in range(1, halves):
                    act(k, piece)

    w_share(lambda k, piece: w_far(k, piece).start())

    blocks = frames * frame_blocks
    key_block = lax.broadcasted_iota(jnp.int32, (blocks, toks), 0)
    query_block = lax.broadcasted_iota(jnp.int32, (blocks, toks), 1) // BLOCK
    term = jnp.full((blocks, toks), -NEG, jnp.float32)
    for b in range(local_blocks):
        used = counts_ref[b]
        for j in range(LIST):
            listed = jnp.where(j < used, lists_ref[b, j], -1)
            term = jnp.where((key_block == listed) & (query_block == b), 0.0, term)
    mbuf[z] = term
    for d in range(1, reps):
        mask_copy((z + d) % reps, z).start()

    for kind in range(3):
        if_extra(lambda slot: start_own(kind, slot))

    for piece in range(pieces):
        w_mate(0, piece).start()
        w_local(piece).start()

    for d in range(1, reps):
        mask_copy(z, (z + d) % reps).wait_recv()

    def pass_on(kind, src, slot):
        z_copy(kind, slot, 0, z, src).wait_recv()
        for e in range(1, frames):
            x_copy(kind, slot, src, e).start()

    def rest(slot):
        for kind in range(3):
            own_copy(kind, slot, my_head(slot)).wait()
        for kind in range(2):
            for rep in range(reps):
                for d in range(1, frames):
                    there = (kbuf, vbuf)[kind].at[slot, (tm - d + frames) % frames, rows(rep)]
                    pltpu.make_async_remote_copy(
                        src_ref=there, dst_ref=there,
                        send_sem=xs.at[kind, slot, rep, d - 1],
                        recv_sem=xr.at[kind, slot, rep, d - 1],
                        device_id={"tm": (tm + d) % frames}, device_id_type=MESH,
                    ).wait_recv()

    tile = min(span, 256)

    def turn_values(slot):
        def turn(frame, _):
            for at in range(0, span, tile):
                part = vbuf[slot, frame, at : at + tile].astype(jnp.float32)
                vturned[slot, frame, :, at : at + tile] = part.T.astype(jnp.bfloat16)
            return 0

        lax.fori_loop(0, frames, turn, 0)

    def attend(slot, chunk):
        queries = qbuf[slot, rows(chunk)]
        factor = 1.4426950408889634 / HD**0.5

        def step(frame, state):
            top, total, sums = state
            terms = mbuf[chunk, pl.ds(pl.multiple_of(frame * frame_blocks, frame_blocks), frame_blocks)]
            tiles = []
            new_top = top
            for at in range(0, span, tile):
                scores = lax.dot_general(
                    kbuf[slot, frame, at : at + tile], queries, (((1,), (1,)), ((), ())),
                    preferred_element_type=jnp.float32,
                )
                own_terms = terms[at // BLOCK : (at + tile) // BLOCK]
                scores = scores.reshape(tile // BLOCK, BLOCK, toks) + own_terms[:, None, :]
                scores = scores.reshape(tile, toks)
                new_top = jnp.maximum(new_top, jnp.max(scores, axis=0, keepdims=True))
                tiles.append(scores)
            scale = jnp.exp2((top - new_top) * factor)
            total = total * scale
            sums = sums * scale
            for n, scores in enumerate(tiles):
                weights = jnp.exp2((scores - new_top) * factor)
                total = total + jnp.sum(weights, axis=0, keepdims=True)
                sums = sums + jnp.dot(
                    vturned[slot, frame, :, n * tile : (n + 1) * tile],
                    weights.astype(jnp.bfloat16),
                    preferred_element_type=jnp.float32,
                )
            return new_top, total, sums

        state = (
            jnp.full((1, toks), -NEG, jnp.float32),
            jnp.zeros((1, toks), jnp.float32),
            jnp.zeros((HD, toks), jnp.float32),
        )
        _, total, sums = lax.fori_loop(0, frames, step, state, unroll=min(frames, 2))
        stage[slot, rows(chunk)] = (sums / total).T.astype(jnp.bfloat16)

    def position(slot, group):
        return slot * groups + group if slot < base else base * groups + extra_rank(z, group)

    def att_copy(slot, chunk):
        return pltpu.make_async_remote_copy(
            src_ref=stage.at[slot, rows(chunk)], dst_ref=abuf.at[z, :, cols(position(slot, g))],
            send_sem=ats.at[slot, chunk], recv_sem=atr.at[slot, g],
            device_id={"heads": chunk}, device_id_type=MESH,
        )

    def att_local(slot):
        return pltpu.make_async_copy(
            stage.at[slot, rows(g)], abuf.at[z, :, cols(position(slot, g))], ats.at[slot, g]
        )

    def arrive(slot, other):
        there = abuf.at[z, :, cols(position(slot, other))]
        pltpu.make_async_remote_copy(
            src_ref=stage.at[slot, rows(g)], dst_ref=there,
            send_sem=ats.at[slot, other], recv_sem=atr.at[slot, other],
            device_id={"heads": other}, device_id_type=MESH,
        ).wait_recv()

    def attend_all(slot, beside=lambda: None):
        def one_chunk(i, _):
            chunk = (z + i) % reps

            @pl.when(i > 0)
            def _():
                z_copy(2, slot, 0, z, chunk).wait_recv()

            attend(slot, chunk)
            pl.when(i == 0)(beside)

            @pl.when(chunk != g)
            def _():
                att_copy(slot, chunk).start()

            @pl.when(chunk == g)
            def _():
                att_local(slot).start()

            return 0

        turn_values(slot)
        lax.fori_loop(0, reps, one_chunk, 0)

    line_cols = (pl.ds(0, base * groups * HD), pl.ds(base * groups * HD, (heads - base * reps) * HD))
    line_parts = 2 if extra else 1

    def line_copy(part, src, way):
        there = abuf.at[src, :, line_cols[part]]
        return pltpu.make_async_remote_copy(
            src_ref=there, dst_ref=there,
            send_sem=gs.at[part, (way + 1) // 2, src], recv_sem=gr.at[part, src],
            device_id={"rep": (z + way + reps) % reps}, device_id_type=MESH,
        )

    def line_start(part):
        @pl.when(z + 1 < reps)
        def _():
            line_copy(part, z, 1).start()

        @pl.when(z > 0)
        def _():
            line_copy(part, z, -1).start()

    def line_relay(part, d):
        @pl.when(z - d >= 0)
        def _():
            src = (z - d + reps) % reps
            line_copy(part, src, 1).wait_recv()

            @pl.when(z + 1 < reps)
            def _():
                line_copy(part, src, 1).start()

        @pl.when(z + d < reps)
        def _():
            src = (z + d) % reps
            line_copy(part, src, -1).wait_recv()

            @pl.when(z > 0)
            def _():
                line_copy(part, src, -1).start()

    for kind in range(2):
        for d in range(1, reps):
            wave(kind, d, lambda copy: copy.wait_send())
            wave(kind + 1, d, lambda copy: copy.start())
        for d in range(1, reps):
            src = (z - d + reps) % reps
            each_base(lambda slot: pass_on(kind, src, slot))
            if_extra(lambda slot: pass_on(kind, src, slot))
    each_base(rest)

    def send_on(k, piece):
        w_far(k, piece).wait_recv()
        for d in range(1, frames):
            w_frame(k, piece, d).start()
        w_mate(k, piece).start()

    each_base(lambda slot: attend_all(slot, lambda: w_share(send_on) if slot == 0 else None))
    each_base(lambda slot: att_local(slot).wait())
    for d in range(1, groups):
        each_base(lambda slot: arrive(slot, (g + d) % groups))
    line_start(0)

    if_extra(rest)
    if_extra(attend_all)
    for d in range(1, reps - 1):
        line_relay(0, d)
        if d == 1 and extra:
            if_extra(lambda slot: att_local(slot).wait())
            for e in range(1, groups):
                other = (g + e) % groups
                pl.when(extra_of(other) < extra)(lambda: arrive(base, other))
            line_start(1)
    if extra:
        for d in range(1, reps - 1):
            line_relay(1, d)

    def to_mate(k, piece):
        w_frame(k, piece, 1).wait_recv()
        w_mate(k, piece).start()

    w_share(to_mate, mine=False)
    for piece in range(pieces):
        for k in range(halves):
            w_mate(k, piece).wait_recv()
        w_local(piece).wait()

    def product(src):
        return jnp.dot(abuf[src], wbuf[src], preferred_element_type=jnp.float32)

    out_ref[...] = product(z)
    for d in range(1, reps):
        if d == reps - 1:
            for part in range(line_parts):
                line_relay(part, d)

        @pl.when(z - d >= 0)
        def _():
            out_ref[...] += product((z - d + reps) % reps)

        @pl.when(z + d < reps)
        def _():
            out_ref[...] += product((z + d) % reps)

    for d in range(1, reps):
        mask_copy((z + d) % reps, z).wait_send()
        wave(2, d, lambda copy: copy.wait_send())

    def sent(slot):
        for kind in range(2):
            for rep in range(reps):
                for d in range(1, frames):
                    x_copy(kind, slot, rep, d).wait_send()
        for d in range(1, groups):
            att_copy(slot, (g + d) % groups).wait_send()

    each_base(sent)
    if_extra(sent)

    def share_sent(k, piece):
        w_far(k, piece).wait_send()
        for d in range(1, frames):
            w_frame(k, piece, d).wait_send()

    w_share(share_sent)
    for piece in range(pieces):
        for k in range(halves):
            w_mate(k, piece).wait_send()

    for part in range(line_parts):
        @pl.when(z + 1 < reps)
        def _():
            for src in range(reps):
                pl.when(src <= z)(lambda: line_copy(part, src, 1).wait_send())

        @pl.when(z > 0)
        def _():
            for src in range(reps):
                pl.when(src >= z)(lambda: line_copy(part, src, -1).wait_send())


def shards(queries, keys, values, block_lists, list_counts, out_weight, gate):
    frames, groups, reps = (lax.axis_size(a) for a in ("tm", "heads", "rep"))
    toks = queries.shape[0]
    heads = queries.shape[1] // HD
    wide = out_weight.shape[1]
    base, extra = heads // reps, heads % reps
    slots = base + (1 if extra else 0)
    assert groups == reps and groups % 2 == 0
    plane_heads = heads * groups // reps
    span = reps * toks
    parts = 2 if wide % 256 == 0 else 1
    dims = (frames, groups, reps, toks, heads, base, extra, parts)
    others = max(frames - 1, 1)
    halves = groups // 2
    far = max(halves - 1, 1)
    pieces = heads * parts
    vmem, smem, hbm = (
        pl.BlockSpec(memory_space=m) for m in (pltpu.VMEM, pltpu.SMEM, pl.ANY)
    )
    dma = pltpu.SemaphoreType.DMA
    scores = slots * span * span * frames
    summed = pl.pallas_call(
        functools.partial(kernel, dims),
        out_shape=jax.ShapeDtypeStruct((toks, wide), jnp.float32),
        in_specs=[hbm, hbm, hbm, smem, smem, hbm],
        out_specs=vmem,
        scratch_shapes=[
            pltpu.VMEM((slots, span, HD), jnp.bfloat16),
            pltpu.VMEM((slots, frames, span, HD), jnp.bfloat16),
            pltpu.VMEM((slots, frames, span, HD), jnp.bfloat16),
            pltpu.VMEM((slots, frames, HD, span), jnp.bfloat16),
            pltpu.VMEM((reps, span * frames // BLOCK, toks), jnp.float32),
            pltpu.VMEM((slots, span, HD), jnp.bfloat16),
            pltpu.VMEM((reps, toks, plane_heads * HD), jnp.bfloat16),
            pltpu.VMEM((reps, plane_heads * HD, wide), jnp.bfloat16),
            dma((3, slots, reps)), dma((3, slots, reps)),
            dma((reps,)), dma((reps,)),
            dma((2, slots, reps, others)), dma((2, slots, reps, others)),
            dma((3, slots)), dma((pieces,)),
            dma((slots, groups)), dma((slots, groups)),
            dma((2, 2, reps)), dma((2, reps)),
            dma((far, pieces)), dma((far, pieces)),
            dma((far, pieces, others)), dma((far, pieces)),
            dma((halves, pieces)), dma((halves, pieces)),
        ],
        compiler_params=pltpu.CompilerParams(
            collective_id=0, has_side_effects=True, vmem_limit_bytes=56 * 2**20
        ),
        cost_estimate=pl.CostEstimate(
            flops=4 * scores * HD + 2 * toks * plane_heads * HD * reps * wide,
            bytes_accessed=2 * (3 * queries.size + out_weight.size),
            transcendentals=scores,
        ),
    )(queries, keys, values, block_lists, list_counts, out_weight)
    return (gate[None, :] * summed).astype(jnp.bfloat16)


def solution(mesh):
    placed = (
        P(("tm", "rep"), "heads"),
        P(("tm", "rep"), "heads"),
        P(("tm", "rep"), "heads"),
        P(("tm", "rep"), None),
        P(("tm", "rep")),
        P("heads", "rep"),
        P("rep"),
    )
    return jax.shard_map(
        shards, mesh=mesh, in_specs=placed, out_specs=P(("tm", "heads"), "rep"), check_vma=False
    )
```

```python
import functools

import jax
import jax.numpy as jnp
from jax import lax
from jax.experimental import pallas as pl
from jax.experimental.pallas import tpu as pltpu
from jax.sharding import PartitionSpec as P

HD = 128
BLOCK = 128
LIST = 16
NEG = 1e30
MESH = pl.DeviceIdType.MESH


def extra_rep(g, reps):
    half = g // 2
    return ((1 - g % 2) * half + (g % 2) * (reps - 1 - half)) % reps


def kernel(
    dims,
    q_ref, k_ref, v_ref, lists_ref, counts_ref, w_ref,
    out_ref,
    qbuf, kbuf, vbuf, vturned, mbuf, stage, abuf, wbuf,
    zs, zr, zms, zmr, xs, xr, own_sem, w_own, ats, atr, gs, gr, wys, wyr, wxs, wxr, wms, wmr,
):
    frames, groups, reps, toks, heads, base, extra, parts = dims
    tm = lax.axis_index("tm")
    g = lax.axis_index("heads")
    z = lax.axis_index("rep")
    span = reps * toks
    local_blocks = toks // BLOCK
    frame_blocks = span // BLOCK
    part_rows = w_ref.shape[0] // parts
    halves = groups // 2

    def cols(head):
        return pl.ds(pl.multiple_of(head * HD, HD), HD)

    def rows(rep):
        return pl.ds(pl.multiple_of(rep * toks, toks), toks)

    def extra_rank(plane, group):
        return sum(
            jnp.where((other < group) & ((plane - extra_rep(other, reps) + reps) % reps < extra), 1, 0)
            for other in range(groups)
        )

    def extra_of(group):
        return (z - extra_rep(group, reps) + reps) % reps

    my_extra = extra_of(g)
    has_extra = my_extra < extra

    def extra_owner(plane, position):
        owner = sum(
            jnp.where(
                ((plane - extra_rep(other, reps) + reps) % reps < extra)
                & (extra_rank(plane, other) == position),
                other,
                0,
            )
            for other in range(groups)
        )
        return owner, base * reps + (plane - extra_rep(owner, reps) + reps) % reps

    barrier = pltpu.get_barrier_semaphore()
    for axis, count, me in (("rep", reps, z), ("tm", frames, tm), ("heads", groups, g)):
        for d in range(1, count):
            pl.semaphore_signal(
                barrier, inc=1, device_id={axis: (me + d) % count}, device_id_type=MESH
            )
    blocks = frames * frame_blocks
    key_block = lax.broadcasted_iota(jnp.int32, (blocks, toks), 0)
    query_block = lax.broadcasted_iota(jnp.int32, (blocks, toks), 1) // BLOCK
    term = jnp.full((blocks, toks), -NEG, jnp.float32)
    for b in range(local_blocks):
        used = counts_ref[b]
        for j in range(LIST):
            listed = jnp.where(j < used, lists_ref[b, j], -1)
            term = jnp.where((key_block == listed) & (query_block == b), 0.0, term)
    mbuf[z] = term
    pl.semaphore_wait(barrier, reps + frames + groups - 3)

    def mask_copy(dst, src):
        return pltpu.make_async_remote_copy(
            src_ref=mbuf.at[src], dst_ref=mbuf.at[src],
            send_sem=zms.at[dst], recv_sem=zmr.at[src],
            device_id={"rep": dst}, device_id_type=MESH,
        )

    sources = (k_ref, v_ref, q_ref)

    def landing(kind, slot, rep):
        if kind == 2:
            return qbuf.at[slot, rows(rep)]
        return (kbuf, vbuf)[kind].at[slot, tm, rows(rep)]

    def z_copy(kind, slot, head, dst, src):
        return pltpu.make_async_remote_copy(
            src_ref=sources[kind].at[:, cols(head)], dst_ref=landing(kind, slot, src),
            send_sem=zs.at[kind, slot, dst], recv_sem=zr.at[kind, slot, src],
            device_id={"rep": dst}, device_id_type=MESH,
        )

    def own_copy(kind, slot, head):
        return pltpu.make_async_copy(
            sources[kind].at[:, cols(head)], landing(kind, slot, z), own_sem.at[kind, slot]
        )

    def x_copy(kind, slot, rep, d, src=None):
        there = landing(kind, slot, rep)
        return pltpu.make_async_remote_copy(
            src_ref=there if src is None else src, dst_ref=there,
            send_sem=xs.at[kind, slot, rep, d - 1], recv_sem=xr.at[kind, slot, rep, d - 1],
            device_id={"tm": (tm + d) % frames}, device_id_type=MESH,
        )

    def my_head(slot):
        return slot * reps + z if slot < base else base * reps + my_extra

    def if_extra(act):
        if extra:
            pl.when(has_extra)(lambda: act(base))

    def each_base(act):
        for slot in range(base):
            act(slot)

    def start_own(kind, slot):
        if kind < 2:
            for d in range(1, frames):
                x_copy(kind, slot, z, d, sources[kind].at[:, cols(my_head(slot))]).start()
        own_copy(kind, slot, my_head(slot)).start()

    def wave(kind, d, act):
        dst = (z + d) % reps
        each_base(lambda slot: act(z_copy(kind, slot, slot * reps + dst, dst, z)))
        for n in range(extra):
            pl.when((extra_rep(g, reps) + n) % reps == dst)(
                lambda: act(z_copy(kind, base, base * reps + n, dst, z))
            )

    for d in range(1, reps):
        wave(0, d, lambda copy: copy.start())
    for kind in range(3):
        each_base(lambda slot: start_own(kind, slot))

    mate = g + 1 - 2 * (g % 2)
    pieces = parts

    def w_here(piece):
        return w_ref.at[pl.ds(piece * part_rows, part_rows)]

    def w_there(group, piece):
        return wbuf.at[group, pl.ds(piece * part_rows, part_rows)]

    def w_far(k, piece):
        return pltpu.make_async_remote_copy(
            src_ref=w_here(piece), dst_ref=w_there(g, piece),
            send_sem=wys.at[k - 1, piece], recv_sem=wyr.at[k - 1, piece],
            device_id={"heads": (g + 2 * k) % groups}, device_id_type=MESH,
        )

    def w_frame(k, piece, d):
        there = w_there((g - 2 * k + groups) % groups, piece)
        return pltpu.make_async_remote_copy(
            src_ref=there, dst_ref=there,
            send_sem=wxs.at[k - 1, piece, d - 1], recv_sem=wxr.at[k - 1, piece],
            device_id={"tm": (tm + d) % frames}, device_id_type=MESH,
        )

    def w_mate(k, piece):
        there = w_there((g - 2 * k + groups) % groups, piece)
        return pltpu.make_async_remote_copy(
            src_ref=there if k else w_here(piece), dst_ref=there,
            send_sem=wms.at[k, piece], recv_sem=wmr.at[k, piece],
            device_id={"heads": mate}, device_id_type=MESH,
        )

    def w_local(piece):
        return pltpu.make_async_copy(w_here(piece), w_there(g, piece), w_own.at[piece])

    def w_share(act, mine=True):
        for piece in range(pieces):
            fetch = tm == piece % frames

            @pl.when(fetch if mine else jnp.logical_not(fetch))
            def _():
                for k in range(1, halves):
                    act(k, piece)

    w_share(lambda k, piece: w_far(k, piece).start())

    for d in range(1, reps):
        mask_copy((z + d) % reps, z).start()

    for kind in range(3):
        if_extra(lambda slot: start_own(kind, slot))

    def pass_on(kind, src, slot):
        z_copy(kind, slot, 0, z, src).wait_recv()
        for e in range(1, frames):
            x_copy(kind, slot, src, e).start()

    def rest(slot):
        for kind in range(3):
            own_copy(kind, slot, my_head(slot)).wait()
        for kind in range(2):
            for rep in range(reps):
                for d in range(1, frames):
                    there = (kbuf, vbuf)[kind].at[slot, (tm - d + frames) % frames, rows(rep)]
                    pltpu.make_async_remote_copy(
                        src_ref=there, dst_ref=there,
                        send_sem=xs.at[kind, slot, rep, d - 1],
                        recv_sem=xr.at[kind, slot, rep, d - 1],
                        device_id={"tm": (tm + d) % frames}, device_id_type=MESH,
                    ).wait_recv()

    tile = min(span, 256)

    def turn_values(slot):
        def turn(frame, _):
            for at in range(0, span, tile):
                part = vbuf[slot, frame, at : at + tile].astype(jnp.float32)
                vturned[slot, frame, :, at : at + tile] = part.T.astype(jnp.bfloat16)
            return 0

        lax.fori_loop(0, frames, turn, 0)

    def attend(slot, chunk):
        queries = qbuf[slot, rows(chunk)]
        factor = 1.4426950408889634 / HD**0.5

        def step(frame, state):
            top, total, sums = state
            terms = mbuf[chunk, pl.ds(pl.multiple_of(frame * frame_blocks, frame_blocks), frame_blocks)]
            tiles = []
            new_top = top
            for at in range(0, span, tile):
                scores = lax.dot_general(
                    kbuf[slot, frame, at : at + tile], queries, (((1,), (1,)), ((), ())),
                    preferred_element_type=jnp.float32,
                )
                own_terms = terms[at // BLOCK : (at + tile) // BLOCK]
                scores = scores.reshape(tile // BLOCK, BLOCK, toks) + own_terms[:, None, :]
                scores = scores.reshape(tile, toks)
                new_top = jnp.maximum(new_top, jnp.max(scores, axis=0, keepdims=True))
                tiles.append(scores)
            scale = jnp.exp2((top - new_top) * factor)
            total = total * scale
            sums = sums * scale
            for n, scores in enumerate(tiles):
                weights = jnp.exp2((scores - new_top) * factor)
                total = total + jnp.sum(weights, axis=0, keepdims=True)
                sums = sums + jnp.dot(
                    vturned[slot, frame, :, n * tile : (n + 1) * tile],
                    weights.astype(jnp.bfloat16),
                    preferred_element_type=jnp.float32,
                )
            return new_top, total, sums

        state = (
            jnp.full((1, toks), -NEG, jnp.float32),
            jnp.zeros((1, toks), jnp.float32),
            jnp.zeros((HD, toks), jnp.float32),
        )
        _, total, sums = lax.fori_loop(0, frames, step, state, unroll=min(frames, 2))
        stage[slot, rows(chunk)] = (sums / total).T.astype(jnp.bfloat16)

    def position(slot, group):
        return slot * groups + group if slot < base else base * groups + extra_rank(z, group)

    def att_copy(slot, chunk):
        return pltpu.make_async_remote_copy(
            src_ref=stage.at[slot, rows(chunk)], dst_ref=abuf.at[z, :, cols(position(slot, g))],
            send_sem=ats.at[slot, chunk], recv_sem=atr.at[slot, g],
            device_id={"heads": chunk}, device_id_type=MESH,
        )

    def att_local(slot):
        return pltpu.make_async_copy(
            stage.at[slot, rows(g)], abuf.at[z, :, cols(position(slot, g))], ats.at[slot, g]
        )

    def arrive(slot, other):
        there = abuf.at[z, :, cols(position(slot, other))]
        pltpu.make_async_remote_copy(
            src_ref=stage.at[slot, rows(g)], dst_ref=there,
            send_sem=ats.at[slot, other], recv_sem=atr.at[slot, other],
            device_id={"heads": other}, device_id_type=MESH,
        ).wait_recv()

    def attend_all(slot, beside=lambda: None):
        def one_chunk(i, _):
            chunk = (z + i) % reps

            @pl.when(i > 0)
            def _():
                z_copy(2, slot, 0, z, chunk).wait_recv()

            attend(slot, chunk)
            pl.when(i == 0)(beside)

            @pl.when(chunk != g)
            def _():
                att_copy(slot, chunk).start()

            @pl.when(chunk == g)
            def _():
                att_local(slot).start()

            return 0

        turn_values(slot)
        lax.fori_loop(0, reps, one_chunk, 0)

    line_cols = (pl.ds(0, base * groups * HD), pl.ds(base * groups * HD, (heads - base * reps) * HD))
    line_parts = 2 if extra else 1

    def line_copy(part, src, way):
        there = abuf.at[src, :, line_cols[part]]
        return pltpu.make_async_remote_copy(
            src_ref=there, dst_ref=there,
            send_sem=gs.at[part, (way + 1) // 2, src], recv_sem=gr.at[part, src],
            device_id={"rep": (z + way + reps) % reps}, device_id_type=MESH,
        )

    def line_start(part):
        @pl.when(z + 1 < reps)
        def _():
            line_copy(part, z, 1).start()

        @pl.when(z > 0)
        def _():
            line_copy(part, z, -1).start()

    def line_relay(part, d):
        @pl.when(z - d >= 0)
        def _():
            src = (z - d + reps) % reps
            line_copy(part, src, 1).wait_recv()

            @pl.when(z + 1 < reps)
            def _():
                line_copy(part, src, 1).start()

        @pl.when(z + d < reps)
        def _():
            src = (z + d) % reps
            line_copy(part, src, -1).wait_recv()

            @pl.when(z > 0)
            def _():
                line_copy(part, src, -1).start()

    for kind in range(2):
        for d in range(1, reps):
            wave(kind, d, lambda copy: copy.wait_send())
            wave(kind + 1, d, lambda copy: copy.start())
        for d in range(1, reps):
            src = (z - d + reps) % reps
            each_base(lambda slot: pass_on(kind, src, slot))
            if_extra(lambda slot: pass_on(kind, src, slot))
    for piece in range(pieces):
        w_mate(0, piece).start()
        w_local(piece).start()

    for d in range(1, reps):
        mask_copy(z, (z + d) % reps).wait_recv()

    each_base(rest)

    def send_on(k, piece):
        w_far(k, piece).wait_recv()
        for d in range(1, frames):
            w_frame(k, piece, d).start()
        w_mate(k, piece).start()

    each_base(lambda slot: attend_all(slot, lambda: w_share(send_on) if slot == 0 else None))
    each_base(lambda slot: att_local(slot).wait())
    for d in range(1, groups):
        each_base(lambda slot: arrive(slot, (g + d) % groups))
    line_start(0)

    def to_mate(k, piece):
        w_frame(k, piece, 1).wait_recv()
        w_mate(k, piece).start()

    if_extra(rest)
    if_extra(attend_all)
    for d in range(1, reps - 1):
        line_relay(0, d)
        if d == 1 and extra:
            if_extra(lambda slot: att_local(slot).wait())
            for e in range(1, groups):
                other = (g + e) % groups
                pl.when(extra_of(other) < extra)(lambda: arrive(base, other))
            line_start(1)
        if d == 1:
            w_share(to_mate, mine=False)
    if extra:
        for d in range(1, reps - 1):
            line_relay(1, d)

    for piece in range(pieces):
        for k in range(halves):
            w_mate(k, piece).wait_recv()
        w_local(piece).wait()

    def product(src):
        total = None
        for at in range(abuf.shape[2] // HD):
            if at < base * groups:
                group, head = at % groups, (at // groups) * reps + src
            else:
                group, head = extra_owner(src, at - base * groups)
            term = jnp.dot(
                abuf[src, :, at * HD : (at + 1) * HD], wbuf[group, cols(head)],
                preferred_element_type=jnp.float32,
            )
            total = term if total is None else total + term
        return total

    out_ref[...] = product(z)
    for d in range(1, reps):
        if d == reps - 1:
            for part in range(line_parts):
                line_relay(part, d)

        @pl.when(z - d >= 0)
        def _():
            out_ref[...] += product((z - d + reps) % reps)

        @pl.when(z + d < reps)
        def _():
            out_ref[...] += product((z + d) % reps)

    for d in range(1, reps):
        mask_copy((z + d) % reps, z).wait_send()
        wave(2, d, lambda copy: copy.wait_send())

    def sent(slot):
        for kind in range(2):
            for rep in range(reps):
                for d in range(1, frames):
                    x_copy(kind, slot, rep, d).wait_send()
        for d in range(1, groups):
            att_copy(slot, (g + d) % groups).wait_send()

    each_base(sent)
    if_extra(sent)

    def share_sent(k, piece):
        w_far(k, piece).wait_send()
        for d in range(1, frames):
            w_frame(k, piece, d).wait_send()

    w_share(share_sent)
    for piece in range(pieces):
        for k in range(halves):
            w_mate(k, piece).wait_send()

    for part in range(line_parts):
        @pl.when(z + 1 < reps)
        def _():
            for src in range(reps):
                pl.when(src <= z)(lambda: line_copy(part, src, 1).wait_send())

        @pl.when(z > 0)
        def _():
            for src in range(reps):
                pl.when(src >= z)(lambda: line_copy(part, src, -1).wait_send())


def shards(queries, keys, values, block_lists, list_counts, out_weight, gate):
    frames, groups, reps = (lax.axis_size(a) for a in ("tm", "heads", "rep"))
    toks = queries.shape[0]
    heads = queries.shape[1] // HD
    wide = out_weight.shape[1]
    base, extra = heads // reps, heads % reps
    slots = base + (1 if extra else 0)
    assert groups == reps and groups % 2 == 0
    plane_heads = heads * groups // reps
    span = reps * toks
    parts = 2 if out_weight.shape[0] % 32 == 0 else 1
    dims = (frames, groups, reps, toks, heads, base, extra, parts)
    others = max(frames - 1, 1)
    halves = groups // 2
    far = max(halves - 1, 1)
    pieces = parts
    vmem, smem, hbm = (
        pl.BlockSpec(memory_space=m) for m in (pltpu.VMEM, pltpu.SMEM, pl.ANY)
    )
    dma = pltpu.SemaphoreType.DMA
    scores = slots * span * span * frames
    summed = pl.pallas_call(
        functools.partial(kernel, dims),
        out_shape=jax.ShapeDtypeStruct((toks, wide), jnp.float32),
        in_specs=[hbm, hbm, hbm, smem, smem, hbm],
        out_specs=vmem,
        scratch_shapes=[
            pltpu.VMEM((slots, span, HD), jnp.bfloat16),
            pltpu.VMEM((slots, frames, span, HD), jnp.bfloat16),
            pltpu.VMEM((slots, frames, span, HD), jnp.bfloat16),
            pltpu.VMEM((slots, frames, HD, span), jnp.bfloat16),
            pltpu.VMEM((reps, span * frames // BLOCK, toks), jnp.float32),
            pltpu.VMEM((slots, span, HD), jnp.bfloat16),
            pltpu.VMEM((reps, toks, plane_heads * HD), jnp.bfloat16),
            pltpu.VMEM((groups, heads * HD, wide), jnp.bfloat16),
            dma((3, slots, reps)), dma((3, slots, reps)),
            dma((reps,)), dma((reps,)),
            dma((2, slots, reps, others)), dma((2, slots, reps, others)),
            dma((3, slots)), dma((pieces,)),
            dma((slots, groups)), dma((slots, groups)),
            dma((2, 2, reps)), dma((2, reps)),
            dma((far, pieces)), dma((far, pieces)),
            dma((far, pieces, others)), dma((far, pieces)),
            dma((halves, pieces)), dma((halves, pieces)),
        ],
        compiler_params=pltpu.CompilerParams(
            collective_id=0, has_side_effects=True, vmem_limit_bytes=56 * 2**20
        ),
        cost_estimate=pl.CostEstimate(
            flops=4 * scores * HD + 2 * toks * plane_heads * HD * reps * wide,
            bytes_accessed=2 * (3 * queries.size + out_weight.size),
            transcendentals=scores,
        ),
    )(queries, keys, values, block_lists, list_counts, out_weight)
    return (gate[None, :] * summed).astype(jnp.bfloat16)


def solution(mesh):
    placed = (
        P(("tm", "rep"), "heads"),
        P(("tm", "rep"), "heads"),
        P(("tm", "rep"), "heads"),
        P(("tm", "rep"), None),
        P(("tm", "rep")),
        P("heads", "rep"),
        P("rep"),
    )
    return jax.shard_map(
        shards, mesh=mesh, in_specs=placed, out_specs=P(("tm", "heads"), "rep"), check_vma=False
    )
```

```python
import functools

import jax
import jax.numpy as jnp
from jax import lax
from jax.experimental import pallas as pl
from jax.experimental.pallas import tpu as pltpu
from jax.sharding import PartitionSpec as P

HD = 128
BLOCK = 128
LIST = 16
NEG = 1e30
MESH = pl.DeviceIdType.MESH


def extra_rep(g, reps):
    half = g // 2
    return ((1 - g % 2) * half + (g % 2) * (reps - 1 - half)) % reps


def kernel(
    dims,
    q_ref, k_ref, v_ref, lists_ref, counts_ref, w_ref,
    out_ref,
    qbuf, kbuf, vbuf, vturned, mbuf, stage, abuf, wbuf,
    zs, zr, zms, zmr, xs, xr, own_sem, w_own, ats, atr, gs, gr, wys, wyr, wxs, wxr, wms, wmr,
):
    frames, groups, reps, toks, heads, base, extra, parts = dims
    tm = lax.axis_index("tm")
    g = lax.axis_index("heads")
    z = lax.axis_index("rep")
    span = reps * toks
    local_blocks = toks // BLOCK
    frame_blocks = span // BLOCK
    part_rows = w_ref.shape[0] // parts
    halves = groups // 2

    def cols(head):
        return pl.ds(pl.multiple_of(head * HD, HD), HD)

    def rows(rep):
        return pl.ds(pl.multiple_of(rep * toks, toks), toks)

    def extra_rank(plane, group):
        return sum(
            jnp.where((other < group) & ((plane - extra_rep(other, reps) + reps) % reps < extra), 1, 0)
            for other in range(groups)
        )

    def extra_of(group):
        return (z - extra_rep(group, reps) + reps) % reps

    my_extra = extra_of(g)
    has_extra = my_extra < extra

    def extra_owner(plane, position):
        owner = sum(
            jnp.where(
                ((plane - extra_rep(other, reps) + reps) % reps < extra)
                & (extra_rank(plane, other) == position),
                other,
                0,
            )
            for other in range(groups)
        )
        return owner, base * reps + (plane - extra_rep(owner, reps) + reps) % reps

    barrier = pltpu.get_barrier_semaphore()
    for axis, count, me in (("rep", reps, z), ("tm", frames, tm), ("heads", groups, g)):
        for d in range(1, count):
            pl.semaphore_signal(
                barrier, inc=1, device_id={axis: (me + d) % count}, device_id_type=MESH
            )
    blocks = frames * frame_blocks
    key_block = lax.broadcasted_iota(jnp.int32, (blocks, toks), 0)
    query_block = lax.broadcasted_iota(jnp.int32, (blocks, toks), 1) // BLOCK
    term = jnp.full((blocks, toks), -NEG, jnp.float32)
    for b in range(local_blocks):
        used = counts_ref[b]
        for j in range(LIST):
            listed = jnp.where(j < used, lists_ref[b, j], -1)
            term = jnp.where((key_block == listed) & (query_block == b), 0.0, term)
    mbuf[z] = term
    pl.semaphore_wait(barrier, reps + frames + groups - 3)

    def mask_copy(dst, src):
        return pltpu.make_async_remote_copy(
            src_ref=mbuf.at[src], dst_ref=mbuf.at[src],
            send_sem=zms.at[dst], recv_sem=zmr.at[src],
            device_id={"rep": dst}, device_id_type=MESH,
        )

    sources = (k_ref, v_ref, q_ref)

    def landing(kind, slot, rep):
        if kind == 2:
            return qbuf.at[slot, rows(rep)]
        return (kbuf, vbuf)[kind].at[slot, tm, rows(rep)]

    def z_copy(kind, slot, head, dst, src):
        return pltpu.make_async_remote_copy(
            src_ref=sources[kind].at[:, cols(head)], dst_ref=landing(kind, slot, src),
            send_sem=zs.at[kind, slot, dst], recv_sem=zr.at[kind, slot, src],
            device_id={"rep": dst}, device_id_type=MESH,
        )

    def own_copy(kind, slot, head):
        return pltpu.make_async_copy(
            sources[kind].at[:, cols(head)], landing(kind, slot, z), own_sem.at[kind, slot]
        )

    def x_copy(kind, slot, rep, d, src=None):
        there = landing(kind, slot, rep)
        return pltpu.make_async_remote_copy(
            src_ref=there if src is None else src, dst_ref=there,
            send_sem=xs.at[kind, slot, rep, d - 1], recv_sem=xr.at[kind, slot, rep, d - 1],
            device_id={"tm": (tm + d) % frames}, device_id_type=MESH,
        )

    def my_head(slot):
        return slot * reps + z if slot < base else base * reps + my_extra

    def if_extra(act):
        if extra:
            pl.when(has_extra)(lambda: act(base))

    def each_base(act):
        for slot in range(base):
            act(slot)

    def start_own(kind, slot):
        if kind < 2:
            for d in range(1, frames):
                x_copy(kind, slot, z, d, sources[kind].at[:, cols(my_head(slot))]).start()
        own_copy(kind, slot, my_head(slot)).start()

    def wave(kind, d, act):
        dst = (z + d) % reps
        each_base(lambda slot: act(z_copy(kind, slot, slot * reps + dst, dst, z)))
        for n in range(extra):
            pl.when((extra_rep(g, reps) + n) % reps == dst)(
                lambda: act(z_copy(kind, base, base * reps + n, dst, z))
            )

    for d in range(1, reps):
        wave(0, d, lambda copy: copy.start())
    for kind in range(3):
        each_base(lambda slot: start_own(kind, slot))

    mate = g + 1 - 2 * (g % 2)
    pieces = parts

    def w_here(piece):
        return w_ref.at[pl.ds(piece * part_rows, part_rows)]

    def w_there(group, piece):
        return wbuf.at[group, pl.ds(piece * part_rows, part_rows)]

    def w_far(k, piece):
        return pltpu.make_async_remote_copy(
            src_ref=w_here(piece), dst_ref=w_there(g, piece),
            send_sem=wys.at[k - 1, piece], recv_sem=wyr.at[k - 1, piece],
            device_id={"heads": (g + 2 * k) % groups}, device_id_type=MESH,
        )

    def w_frame(k, piece, d):
        there = w_there((g - 2 * k + groups) % groups, piece)
        return pltpu.make_async_remote_copy(
            src_ref=there, dst_ref=there,
            send_sem=wxs.at[k - 1, piece, d - 1], recv_sem=wxr.at[k - 1, piece],
            device_id={"tm": (tm + d) % frames}, device_id_type=MESH,
        )

    def w_mate(k, piece):
        there = w_there((g - 2 * k + groups) % groups, piece)
        return pltpu.make_async_remote_copy(
            src_ref=there if k else w_here(piece), dst_ref=there,
            send_sem=wms.at[k, piece], recv_sem=wmr.at[k, piece],
            device_id={"heads": mate}, device_id_type=MESH,
        )

    def w_local(piece):
        return pltpu.make_async_copy(w_here(piece), w_there(g, piece), w_own.at[piece])

    def w_share(act, mine=True):
        for piece in range(pieces):
            fetch = tm == piece % frames

            @pl.when(fetch if mine else jnp.logical_not(fetch))
            def _():
                for k in range(1, halves):
                    act(k, piece)

    w_share(lambda k, piece: w_far(k, piece).start())

    for d in range(1, reps):
        mask_copy((z + d) % reps, z).start()

    for kind in range(3):
        if_extra(lambda slot: start_own(kind, slot))

    def pass_on(kind, src, slot):
        z_copy(kind, slot, 0, z, src).wait_recv()
        for e in range(1, frames):
            x_copy(kind, slot, src, e).start()

    def rest(slot):
        for kind in range(3):
            own_copy(kind, slot, my_head(slot)).wait()
        for kind in range(2):
            for rep in range(reps):
                for d in range(1, frames):
                    there = (kbuf, vbuf)[kind].at[slot, (tm - d + frames) % frames, rows(rep)]
                    pltpu.make_async_remote_copy(
                        src_ref=there, dst_ref=there,
                        send_sem=xs.at[kind, slot, rep, d - 1],
                        recv_sem=xr.at[kind, slot, rep, d - 1],
                        device_id={"tm": (tm + d) % frames}, device_id_type=MESH,
                    ).wait_recv()

    tile = min(span, 256)

    def turn_values(slot):
        def turn(frame, _):
            for at in range(0, span, tile):
                part = vbuf[slot, frame, at : at + tile].astype(jnp.float32)
                vturned[slot, frame, :, at : at + tile] = part.T.astype(jnp.bfloat16)
            return 0

        lax.fori_loop(0, frames, turn, 0)

    def attend(slot, chunk):
        queries = qbuf[slot, rows(chunk)]
        factor = 1.4426950408889634 / HD**0.5

        def step(frame, state):
            top, total, sums = state
            terms = mbuf[chunk, pl.ds(pl.multiple_of(frame * frame_blocks, frame_blocks), frame_blocks)]
            tiles = []
            new_top = top
            for at in range(0, span, tile):
                scores = lax.dot_general(
                    kbuf[slot, frame, at : at + tile], queries, (((1,), (1,)), ((), ())),
                    preferred_element_type=jnp.float32,
                )
                own_terms = terms[at // BLOCK : (at + tile) // BLOCK]
                scores = scores.reshape(tile // BLOCK, BLOCK, toks) + own_terms[:, None, :]
                scores = scores.reshape(tile, toks)
                new_top = jnp.maximum(new_top, jnp.max(scores, axis=0, keepdims=True))
                tiles.append(scores)
            scale = jnp.exp2((top - new_top) * factor)
            total = total * scale
            sums = sums * scale
            for n, scores in enumerate(tiles):
                weights = jnp.exp2((scores - new_top) * factor)
                total = total + jnp.sum(weights, axis=0, keepdims=True)
                sums = sums + jnp.dot(
                    vturned[slot, frame, :, n * tile : (n + 1) * tile],
                    weights.astype(jnp.bfloat16),
                    preferred_element_type=jnp.float32,
                )
            return new_top, total, sums

        state = (
            jnp.full((1, toks), -NEG, jnp.float32),
            jnp.zeros((1, toks), jnp.float32),
            jnp.zeros((HD, toks), jnp.float32),
        )
        _, total, sums = lax.fori_loop(0, frames, step, state, unroll=min(frames, 2))
        stage[slot, rows(chunk)] = (sums / total).T.astype(jnp.bfloat16)

    def position(slot, group):
        return slot * groups + group if slot < base else base * groups + extra_rank(z, group)

    def att_copy(slot, chunk):
        return pltpu.make_async_remote_copy(
            src_ref=stage.at[slot, rows(chunk)], dst_ref=abuf.at[z, :, cols(position(slot, g))],
            send_sem=ats.at[slot, chunk], recv_sem=atr.at[slot, g],
            device_id={"heads": chunk}, device_id_type=MESH,
        )

    def att_local(slot):
        return pltpu.make_async_copy(
            stage.at[slot, rows(g)], abuf.at[z, :, cols(position(slot, g))], ats.at[slot, g]
        )

    def arrive(slot, other):
        there = abuf.at[z, :, cols(position(slot, other))]
        pltpu.make_async_remote_copy(
            src_ref=stage.at[slot, rows(g)], dst_ref=there,
            send_sem=ats.at[slot, other], recv_sem=atr.at[slot, other],
            device_id={"heads": other}, device_id_type=MESH,
        ).wait_recv()

    def attend_all(slot, beside=lambda: None):
        def one_chunk(i, _):
            chunk = (z + i) % reps

            @pl.when(i > 0)
            def _():
                z_copy(2, slot, 0, z, chunk).wait_recv()

            attend(slot, chunk)
            pl.when(i == 0)(beside)

            @pl.when(chunk != g)
            def _():
                att_copy(slot, chunk).start()

            @pl.when(chunk == g)
            def _():
                att_local(slot).start()

            return 0

        turn_values(slot)
        lax.fori_loop(0, reps, one_chunk, 0)

    line_cols = (pl.ds(0, base * groups * HD), pl.ds(base * groups * HD, (heads - base * reps) * HD))
    line_parts = 2 if extra else 1

    def line_copy(part, src, way):
        there = abuf.at[src, :, line_cols[part]]
        return pltpu.make_async_remote_copy(
            src_ref=there, dst_ref=there,
            send_sem=gs.at[part, (way + 1) // 2, src], recv_sem=gr.at[part, src],
            device_id={"rep": (z + way + reps) % reps}, device_id_type=MESH,
        )

    def line_start(part):
        @pl.when(z + 1 < reps)
        def _():
            line_copy(part, z, 1).start()

        @pl.when(z > 0)
        def _():
            line_copy(part, z, -1).start()

    def line_relay(part, d):
        @pl.when(z - d >= 0)
        def _():
            src = (z - d + reps) % reps
            line_copy(part, src, 1).wait_recv()

            @pl.when(z + 1 < reps)
            def _():
                line_copy(part, src, 1).start()

        @pl.when(z + d < reps)
        def _():
            src = (z + d) % reps
            line_copy(part, src, -1).wait_recv()

            @pl.when(z > 0)
            def _():
                line_copy(part, src, -1).start()

    for kind in range(2):
        for d in range(1, reps):
            wave(kind, d, lambda copy: copy.wait_send())
            wave(kind + 1, d, lambda copy: copy.start())
        for d in range(1, reps):
            src = (z - d + reps) % reps
            each_base(lambda slot: pass_on(kind, src, slot))
            if_extra(lambda slot: pass_on(kind, src, slot))
    for piece in range(pieces):
        w_mate(0, piece).start()
        w_local(piece).start()

    for d in range(1, reps):
        mask_copy(z, (z + d) % reps).wait_recv()

    each_base(rest)

    def send_on(k, piece):
        w_far(k, piece).wait_recv()
        for d in range(1, frames):
            w_frame(k, piece, d).start()
        w_mate(k, piece).start()

    each_base(lambda slot: attend_all(slot, lambda: w_share(send_on) if slot == 0 else None))
    each_base(lambda slot: att_local(slot).wait())
    for d in range(1, groups):
        each_base(lambda slot: arrive(slot, (g + d) % groups))
    line_start(0)

    def to_mate(k, piece):
        w_frame(k, piece, 1).wait_recv()
        w_mate(k, piece).start()

    if_extra(rest)
    if_extra(attend_all)
    for d in range(1, reps - 1):
        line_relay(0, d)
    if extra:
        if_extra(lambda slot: att_local(slot).wait())
        for e in range(1, groups):
            other = (g + e) % groups
            pl.when(extra_of(other) < extra)(lambda: arrive(base, other))
        line_start(1)
        for d in range(1, reps - 1):
            line_relay(1, d)
    w_share(to_mate, mine=False)
    for piece in range(pieces):
        for k in range(halves):
            w_mate(k, piece).wait_recv()
        w_local(piece).wait()

    def product(src):
        total = None
        for at in range(abuf.shape[2] // HD):
            if at < base * groups:
                group, head = at % groups, (at // groups) * reps + src
            else:
                group, head = extra_owner(src, at - base * groups)
            term = jnp.dot(
                abuf[src, :, at * HD : (at + 1) * HD], wbuf[group, cols(head)],
                preferred_element_type=jnp.float32,
            )
            total = term if total is None else total + term
        return total

    out_ref[...] = product(z)
    for d in range(1, reps):
        if d == reps - 1:
            for part in range(line_parts):
                line_relay(part, d)

        @pl.when(z - d >= 0)
        def _():
            out_ref[...] += product((z - d + reps) % reps)

        @pl.when(z + d < reps)
        def _():
            out_ref[...] += product((z + d) % reps)

    for d in range(1, reps):
        mask_copy((z + d) % reps, z).wait_send()
        wave(2, d, lambda copy: copy.wait_send())

    def sent(slot):
        for kind in range(2):
            for rep in range(reps):
                for d in range(1, frames):
                    x_copy(kind, slot, rep, d).wait_send()
        for d in range(1, groups):
            att_copy(slot, (g + d) % groups).wait_send()

    each_base(sent)
    if_extra(sent)

    def share_sent(k, piece):
        w_far(k, piece).wait_send()
        for d in range(1, frames):
            w_frame(k, piece, d).wait_send()

    w_share(share_sent)
    for piece in range(pieces):
        for k in range(halves):
            w_mate(k, piece).wait_send()

    for part in range(line_parts):
        @pl.when(z + 1 < reps)
        def _():
            for src in range(reps):
                pl.when(src <= z)(lambda: line_copy(part, src, 1).wait_send())

        @pl.when(z > 0)
        def _():
            for src in range(reps):
                pl.when(src >= z)(lambda: line_copy(part, src, -1).wait_send())


def shards(queries, keys, values, block_lists, list_counts, out_weight, gate):
    frames, groups, reps = (lax.axis_size(a) for a in ("tm", "heads", "rep"))
    toks = queries.shape[0]
    heads = queries.shape[1] // HD
    wide = out_weight.shape[1]
    base, extra = heads // reps, heads % reps
    slots = base + (1 if extra else 0)
    assert groups == reps and groups % 2 == 0
    plane_heads = heads * groups // reps
    span = reps * toks
    parts = 2 if out_weight.shape[0] % 32 == 0 else 1
    dims = (frames, groups, reps, toks, heads, base, extra, parts)
    others = max(frames - 1, 1)
    halves = groups // 2
    far = max(halves - 1, 1)
    pieces = parts
    vmem, smem, hbm = (
        pl.BlockSpec(memory_space=m) for m in (pltpu.VMEM, pltpu.SMEM, pl.ANY)
    )
    dma = pltpu.SemaphoreType.DMA
    scores = slots * span * span * frames
    summed = pl.pallas_call(
        functools.partial(kernel, dims),
        out_shape=jax.ShapeDtypeStruct((toks, wide), jnp.float32),
        in_specs=[hbm, hbm, hbm, smem, smem, hbm],
        out_specs=vmem,
        scratch_shapes=[
            pltpu.VMEM((slots, span, HD), jnp.bfloat16),
            pltpu.VMEM((slots, frames, span, HD), jnp.bfloat16),
            pltpu.VMEM((slots, frames, span, HD), jnp.bfloat16),
            pltpu.VMEM((slots, frames, HD, span), jnp.bfloat16),
            pltpu.VMEM((reps, span * frames // BLOCK, toks), jnp.float32),
            pltpu.VMEM((slots, span, HD), jnp.bfloat16),
            pltpu.VMEM((reps, toks, plane_heads * HD), jnp.bfloat16),
            pltpu.VMEM((groups, heads * HD, wide), jnp.bfloat16),
            dma((3, slots, reps)), dma((3, slots, reps)),
            dma((reps,)), dma((reps,)),
            dma((2, slots, reps, others)), dma((2, slots, reps, others)),
            dma((3, slots)), dma((pieces,)),
            dma((slots, groups)), dma((slots, groups)),
            dma((2, 2, reps)), dma((2, reps)),
            dma((far, pieces)), dma((far, pieces)),
            dma((far, pieces, others)), dma((far, pieces)),
            dma((halves, pieces)), dma((halves, pieces)),
        ],
        compiler_params=pltpu.CompilerParams(
            collective_id=0, has_side_effects=True, vmem_limit_bytes=56 * 2**20
        ),
        cost_estimate=pl.CostEstimate(
            flops=4 * scores * HD + 2 * toks * plane_heads * HD * reps * wide,
            bytes_accessed=2 * (3 * queries.size + out_weight.size),
            transcendentals=scores,
        ),
    )(queries, keys, values, block_lists, list_counts, out_weight)
    return (gate[None, :] * summed).astype(jnp.bfloat16)


def solution(mesh):
    placed = (
        P(("tm", "rep"), "heads"),
        P(("tm", "rep"), "heads"),
        P(("tm", "rep"), "heads"),
        P(("tm", "rep"), None),
        P(("tm", "rep")),
        P("heads", "rep"),
        P("rep"),
    )
    return jax.shard_map(
        shards, mesh=mesh, in_specs=placed, out_specs=P(("tm", "heads"), "rep"), check_vma=False
    )
```

```python
import functools

import jax
import jax.numpy as jnp
from jax import lax
from jax.experimental import pallas as pl
from jax.experimental.pallas import tpu as pltpu
from jax.sharding import PartitionSpec as P

HD = 128
BLOCK = 128
LIST = 16
NEG = 1e30
MESH = pl.DeviceIdType.MESH


def extra_rep(g, reps):
    half = g // 2
    return ((1 - g % 2) * half + (g % 2) * (reps - 1 - half)) % reps


def kernel(
    dims,
    q_ref, k_ref, v_ref, lists_ref, counts_ref, w_ref,
    out_ref,
    qbuf, kbuf, vbuf, vturned, mbuf, stage, abuf, wbuf,
    zs, zr, zms, zmr, xs, xr, own_sem, w_own, ats, atr, gs, gr, wys, wyr, wxs, wxr, wms, wmr,
):
    frames, groups, reps, toks, heads, base, extra, parts = dims
    tm = lax.axis_index("tm")
    g = lax.axis_index("heads")
    z = lax.axis_index("rep")
    span = reps * toks
    local_blocks = toks // BLOCK
    frame_blocks = span // BLOCK
    part_rows = w_ref.shape[0] // parts
    halves = groups // 2

    def cols(head):
        return pl.ds(pl.multiple_of(head * HD, HD), HD)

    def rows(rep):
        return pl.ds(pl.multiple_of(rep * toks, toks), toks)

    def extra_rank(plane, group):
        return sum(
            jnp.where((other < group) & ((plane - extra_rep(other, reps) + reps) % reps < extra), 1, 0)
            for other in range(groups)
        )

    def extra_of(group):
        return (z - extra_rep(group, reps) + reps) % reps

    my_extra = extra_of(g)
    has_extra = my_extra < extra

    def extra_owner(plane, position):
        owner = sum(
            jnp.where(
                ((plane - extra_rep(other, reps) + reps) % reps < extra)
                & (extra_rank(plane, other) == position),
                other,
                0,
            )
            for other in range(groups)
        )
        return owner, base * reps + (plane - extra_rep(owner, reps) + reps) % reps

    barrier = pltpu.get_barrier_semaphore()
    for axis, count, me in (("rep", reps, z), ("tm", frames, tm), ("heads", groups, g)):
        for d in range(1, count):
            pl.semaphore_signal(
                barrier, inc=1, device_id={axis: (me + d) % count}, device_id_type=MESH
            )
    blocks = frames * frame_blocks
    key_block = lax.broadcasted_iota(jnp.int32, (blocks, toks), 0)
    query_block = lax.broadcasted_iota(jnp.int32, (blocks, toks), 1) // BLOCK
    term = jnp.full((blocks, toks), -NEG, jnp.float32)
    for b in range(local_blocks):
        used = counts_ref[b]
        for j in range(LIST):
            listed = jnp.where(j < used, lists_ref[b, j], -1)
            term = jnp.where((key_block == listed) & (query_block == b), 0.0, term)
    mbuf[z] = term
    pl.semaphore_wait(barrier, reps + frames + groups - 3)

    def mask_copy(dst, src):
        return pltpu.make_async_remote_copy(
            src_ref=mbuf.at[src], dst_ref=mbuf.at[src],
            send_sem=zms.at[dst], recv_sem=zmr.at[src],
            device_id={"rep": dst}, device_id_type=MESH,
        )

    sources = (k_ref, v_ref, q_ref)

    def landing(kind, slot, rep):
        if kind == 2:
            return qbuf.at[slot, rows(rep)]
        return (kbuf, vbuf)[kind].at[slot, tm, rows(rep)]

    def z_copy(kind, slot, head, dst, src):
        return pltpu.make_async_remote_copy(
            src_ref=sources[kind].at[:, cols(head)], dst_ref=landing(kind, slot, src),
            send_sem=zs.at[kind, slot, dst], recv_sem=zr.at[kind, slot, src],
            device_id={"rep": dst}, device_id_type=MESH,
        )

    def own_copy(kind, slot, head):
        return pltpu.make_async_copy(
            sources[kind].at[:, cols(head)], landing(kind, slot, z), own_sem.at[kind, slot]
        )

    def x_copy(kind, slot, rep, d, src=None):
        there = landing(kind, slot, rep)
        return pltpu.make_async_remote_copy(
            src_ref=there if src is None else src, dst_ref=there,
            send_sem=xs.at[kind, slot, rep, d - 1], recv_sem=xr.at[kind, slot, rep, d - 1],
            device_id={"tm": (tm + d) % frames}, device_id_type=MESH,
        )

    def my_head(slot):
        return slot * reps + z if slot < base else base * reps + my_extra

    def if_extra(act):
        if extra:
            pl.when(has_extra)(lambda: act(base))

    def each_base(act):
        for slot in range(base):
            act(slot)

    def start_own(kind, slot):
        if kind < 2:
            for d in range(1, frames):
                x_copy(kind, slot, z, d, sources[kind].at[:, cols(my_head(slot))]).start()
        own_copy(kind, slot, my_head(slot)).start()

    def wave(kind, d, act):
        dst = (z + d) % reps
        each_base(lambda slot: act(z_copy(kind, slot, slot * reps + dst, dst, z)))
        for n in range(extra):
            pl.when((extra_rep(g, reps) + n) % reps == dst)(
                lambda: act(z_copy(kind, base, base * reps + n, dst, z))
            )

    for d in range(1, reps):
        wave(0, d, lambda copy: copy.start())
    for kind in range(3):
        each_base(lambda slot: start_own(kind, slot))

    mate = g + 1 - 2 * (g % 2)
    pieces = parts

    def w_here(piece):
        return w_ref.at[pl.ds(piece * part_rows, part_rows)]

    def w_there(group, piece):
        return wbuf.at[group, pl.ds(piece * part_rows, part_rows)]

    def w_far(k, piece):
        return pltpu.make_async_remote_copy(
            src_ref=w_here(piece), dst_ref=w_there(g, piece),
            send_sem=wys.at[k - 1, piece], recv_sem=wyr.at[k - 1, piece],
            device_id={"heads": (g + 2 * k) % groups}, device_id_type=MESH,
        )

    def w_frame(k, piece, d):
        there = w_there((g - 2 * k + groups) % groups, piece)
        return pltpu.make_async_remote_copy(
            src_ref=there, dst_ref=there,
            send_sem=wxs.at[k - 1, piece, d - 1], recv_sem=wxr.at[k - 1, piece],
            device_id={"tm": (tm + d) % frames}, device_id_type=MESH,
        )

    def w_mate(k, piece):
        there = w_there((g - 2 * k + groups) % groups, piece)
        return pltpu.make_async_remote_copy(
            src_ref=there if k else w_here(piece), dst_ref=there,
            send_sem=wms.at[k, piece], recv_sem=wmr.at[k, piece],
            device_id={"heads": mate}, device_id_type=MESH,
        )

    def w_local(piece):
        return pltpu.make_async_copy(w_here(piece), w_there(g, piece), w_own.at[piece])

    def w_share(act, mine=True):
        for piece in range(pieces):
            fetch = tm == piece % frames

            @pl.when(fetch if mine else jnp.logical_not(fetch))
            def _():
                for k in range(1, halves):
                    act(k, piece)

    w_share(lambda k, piece: w_far(k, piece).start())

    for d in range(1, reps):
        mask_copy((z + d) % reps, z).start()

    for kind in range(3):
        if_extra(lambda slot: start_own(kind, slot))

    def pass_on(kind, src, slot):
        z_copy(kind, slot, 0, z, src).wait_recv()
        for e in range(1, frames):
            x_copy(kind, slot, src, e).start()

    def rest(slot):
        for kind in range(3):
            own_copy(kind, slot, my_head(slot)).wait()
        for kind in range(2):
            for rep in range(reps):
                for d in range(1, frames):
                    there = (kbuf, vbuf)[kind].at[slot, (tm - d + frames) % frames, rows(rep)]
                    pltpu.make_async_remote_copy(
                        src_ref=there, dst_ref=there,
                        send_sem=xs.at[kind, slot, rep, d - 1],
                        recv_sem=xr.at[kind, slot, rep, d - 1],
                        device_id={"tm": (tm + d) % frames}, device_id_type=MESH,
                    ).wait_recv()

    tile = min(span, 256)

    def turn_values(slot):
        def turn(frame, _):
            for at in range(0, span, tile):
                part = vbuf[slot, frame, at : at + tile].astype(jnp.float32)
                vturned[slot, frame, :, at : at + tile] = part.T.astype(jnp.bfloat16)
            return 0

        lax.fori_loop(0, frames, turn, 0)

    def attend(slot, chunk):
        queries = qbuf[slot, rows(chunk)]
        factor = 1.4426950408889634 / HD**0.5

        def step(frame, state):
            top, total, sums = state
            terms = mbuf[chunk, pl.ds(pl.multiple_of(frame * frame_blocks, frame_blocks), frame_blocks)]
            tiles = []
            new_top = top
            for at in range(0, span, tile):
                scores = lax.dot_general(
                    kbuf[slot, frame, at : at + tile], queries, (((1,), (1,)), ((), ())),
                    preferred_element_type=jnp.float32,
                )
                own_terms = terms[at // BLOCK : (at + tile) // BLOCK]
                scores = scores.reshape(tile // BLOCK, BLOCK, toks) + own_terms[:, None, :]
                scores = scores.reshape(tile, toks)
                new_top = jnp.maximum(new_top, jnp.max(scores, axis=0, keepdims=True))
                tiles.append(scores)
            scale = jnp.exp2((top - new_top) * factor)
            total = total * scale
            sums = sums * scale
            for n, scores in enumerate(tiles):
                weights = jnp.exp2((scores - new_top) * factor)
                total = total + jnp.sum(weights, axis=0, keepdims=True)
                sums = sums + jnp.dot(
                    vturned[slot, frame, :, n * tile : (n + 1) * tile],
                    weights.astype(jnp.bfloat16),
                    preferred_element_type=jnp.float32,
                )
            return new_top, total, sums

        state = (
            jnp.full((1, toks), -NEG, jnp.float32),
            jnp.zeros((1, toks), jnp.float32),
            jnp.zeros((HD, toks), jnp.float32),
        )
        _, total, sums = lax.fori_loop(0, frames, step, state, unroll=min(frames, 2))
        stage[slot, rows(chunk)] = (sums / total).T.astype(jnp.bfloat16)

    def position(slot, group):
        return slot * groups + group if slot < base else base * groups + extra_rank(z, group)

    def att_copy(slot, chunk):
        return pltpu.make_async_remote_copy(
            src_ref=stage.at[slot, rows(chunk)], dst_ref=abuf.at[z, :, cols(position(slot, g))],
            send_sem=ats.at[slot, chunk], recv_sem=atr.at[slot, g],
            device_id={"heads": chunk}, device_id_type=MESH,
        )

    def att_local(slot):
        return pltpu.make_async_copy(
            stage.at[slot, rows(g)], abuf.at[z, :, cols(position(slot, g))], ats.at[slot, g]
        )

    def arrive(slot, other):
        there = abuf.at[z, :, cols(position(slot, other))]
        pltpu.make_async_remote_copy(
            src_ref=stage.at[slot, rows(g)], dst_ref=there,
            send_sem=ats.at[slot, other], recv_sem=atr.at[slot, other],
            device_id={"heads": other}, device_id_type=MESH,
        ).wait_recv()

    def attend_all(slot, beside=lambda: None):
        def one_chunk(i, _):
            chunk = (z + i) % reps

            @pl.when(i > 0)
            def _():
                z_copy(2, slot, 0, z, chunk).wait_recv()

            attend(slot, chunk)
            pl.when(i == 0)(beside)

            @pl.when(chunk != g)
            def _():
                att_copy(slot, chunk).start()

            @pl.when(chunk == g)
            def _():
                att_local(slot).start()

            return 0

        turn_values(slot)
        lax.fori_loop(0, reps, one_chunk, 0)

    line_cols = (pl.ds(0, base * groups * HD), pl.ds(base * groups * HD, (heads - base * reps) * HD))
    line_parts = 2 if extra else 1

    def line_copy(part, src, way):
        there = abuf.at[src, :, line_cols[part]]
        return pltpu.make_async_remote_copy(
            src_ref=there, dst_ref=there,
            send_sem=gs.at[part, (way + 1) // 2, src], recv_sem=gr.at[part, src],
            device_id={"rep": (z + way + reps) % reps}, device_id_type=MESH,
        )

    def line_start(part):
        @pl.when(z + 1 < reps)
        def _():
            line_copy(part, z, 1).start()

        @pl.when(z > 0)
        def _():
            line_copy(part, z, -1).start()

    def line_relay(part, d):
        @pl.when(z - d >= 0)
        def _():
            src = (z - d + reps) % reps
            line_copy(part, src, 1).wait_recv()

            @pl.when(z + 1 < reps)
            def _():
                line_copy(part, src, 1).start()

        @pl.when(z + d < reps)
        def _():
            src = (z + d) % reps
            line_copy(part, src, -1).wait_recv()

            @pl.when(z > 0)
            def _():
                line_copy(part, src, -1).start()

    for kind in range(2):
        for d in range(1, reps):
            wave(kind, d, lambda copy: copy.wait_send())
            wave(kind + 1, d, lambda copy: copy.start())
        for d in range(1, reps):
            src = (z - d + reps) % reps
            each_base(lambda slot: pass_on(kind, src, slot))
            if_extra(lambda slot: pass_on(kind, src, slot))
    for piece in range(pieces):
        w_mate(0, piece).start()
        w_local(piece).start()

    for d in range(1, reps):
        mask_copy(z, (z + d) % reps).wait_recv()

    each_base(rest)

    def send_on(k, piece):
        w_far(k, piece).wait_recv()
        for d in range(1, frames):
            w_frame(k, piece, d).start()
        w_mate(k, piece).start()

    each_base(lambda slot: attend_all(slot, lambda: w_share(send_on) if slot == 0 else None))
    each_base(lambda slot: att_local(slot).wait())
    for d in range(1, groups):
        each_base(lambda slot: arrive(slot, (g + d) % groups))
    line_start(0)

    def to_mate(k, piece):
        w_frame(k, piece, 1).wait_recv()
        w_mate(k, piece).start()

    if_extra(rest)
    if_extra(attend_all)
    if extra:
        if_extra(lambda slot: att_local(slot).wait())
        for e in range(1, groups):
            other = (g + e) % groups
            pl.when(extra_of(other) < extra)(lambda: arrive(base, other))
        line_start(1)
    for d in range(1, reps - 1):
        for part in range(line_parts):
            line_relay(part, d)
    w_share(to_mate, mine=False)
    for piece in range(pieces):
        for k in range(halves):
            w_mate(k, piece).wait_recv()
        w_local(piece).wait()

    def product(src):
        total = None
        for at in range(abuf.shape[2] // HD):
            if at < base * groups:
                group, head = at % groups, (at // groups) * reps + src
            else:
                group, head = extra_owner(src, at - base * groups)
            term = jnp.dot(
                abuf[src, :, at * HD : (at + 1) * HD], wbuf[group, cols(head)],
                preferred_element_type=jnp.float32,
            )
            total = term if total is None else total + term
        return total

    out_ref[...] = product(z)
    for d in range(1, reps):
        if d == reps - 1:
            for part in range(line_parts):
                line_relay(part, d)

        @pl.when(z - d >= 0)
        def _():
            out_ref[...] += product((z - d + reps) % reps)

        @pl.when(z + d < reps)
        def _():
            out_ref[...] += product((z + d) % reps)

    for d in range(1, reps):
        mask_copy((z + d) % reps, z).wait_send()
        wave(2, d, lambda copy: copy.wait_send())

    def sent(slot):
        for kind in range(2):
            for rep in range(reps):
                for d in range(1, frames):
                    x_copy(kind, slot, rep, d).wait_send()
        for d in range(1, groups):
            att_copy(slot, (g + d) % groups).wait_send()

    each_base(sent)
    if_extra(sent)

    def share_sent(k, piece):
        w_far(k, piece).wait_send()
        for d in range(1, frames):
            w_frame(k, piece, d).wait_send()

    w_share(share_sent)
    for piece in range(pieces):
        for k in range(halves):
            w_mate(k, piece).wait_send()

    for part in range(line_parts):
        @pl.when(z + 1 < reps)
        def _():
            for src in range(reps):
                pl.when(src <= z)(lambda: line_copy(part, src, 1).wait_send())

        @pl.when(z > 0)
        def _():
            for src in range(reps):
                pl.when(src >= z)(lambda: line_copy(part, src, -1).wait_send())


def shards(queries, keys, values, block_lists, list_counts, out_weight, gate):
    frames, groups, reps = (lax.axis_size(a) for a in ("tm", "heads", "rep"))
    toks = queries.shape[0]
    heads = queries.shape[1] // HD
    wide = out_weight.shape[1]
    base, extra = heads // reps, heads % reps
    slots = base + (1 if extra else 0)
    assert groups == reps and groups % 2 == 0
    plane_heads = heads * groups // reps
    span = reps * toks
    parts = 2 if out_weight.shape[0] % 32 == 0 else 1
    dims = (frames, groups, reps, toks, heads, base, extra, parts)
    others = max(frames - 1, 1)
    halves = groups // 2
    far = max(halves - 1, 1)
    pieces = parts
    vmem, smem, hbm = (
        pl.BlockSpec(memory_space=m) for m in (pltpu.VMEM, pltpu.SMEM, pl.ANY)
    )
    dma = pltpu.SemaphoreType.DMA
    scores = slots * span * span * frames
    summed = pl.pallas_call(
        functools.partial(kernel, dims),
        out_shape=jax.ShapeDtypeStruct((toks, wide), jnp.float32),
        in_specs=[hbm, hbm, hbm, smem, smem, hbm],
        out_specs=vmem,
        scratch_shapes=[
            pltpu.VMEM((slots, span, HD), jnp.bfloat16),
            pltpu.VMEM((slots, frames, span, HD), jnp.bfloat16),
            pltpu.VMEM((slots, frames, span, HD), jnp.bfloat16),
            pltpu.VMEM((slots, frames, HD, span), jnp.bfloat16),
            pltpu.VMEM((reps, span * frames // BLOCK, toks), jnp.float32),
            pltpu.VMEM((slots, span, HD), jnp.bfloat16),
            pltpu.VMEM((reps, toks, plane_heads * HD), jnp.bfloat16),
            pltpu.VMEM((groups, heads * HD, wide), jnp.bfloat16),
            dma((3, slots, reps)), dma((3, slots, reps)),
            dma((reps,)), dma((reps,)),
            dma((2, slots, reps, others)), dma((2, slots, reps, others)),
            dma((3, slots)), dma((pieces,)),
            dma((slots, groups)), dma((slots, groups)),
            dma((2, 2, reps)), dma((2, reps)),
            dma((far, pieces)), dma((far, pieces)),
            dma((far, pieces, others)), dma((far, pieces)),
            dma((halves, pieces)), dma((halves, pieces)),
        ],
        compiler_params=pltpu.CompilerParams(
            collective_id=0, has_side_effects=True, vmem_limit_bytes=56 * 2**20
        ),
        cost_estimate=pl.CostEstimate(
            flops=4 * scores * HD + 2 * toks * plane_heads * HD * reps * wide,
            bytes_accessed=2 * (3 * queries.size + out_weight.size),
            transcendentals=scores,
        ),
    )(queries, keys, values, block_lists, list_counts, out_weight)
    return (gate[None, :] * summed).astype(jnp.bfloat16)


def solution(mesh):
    placed = (
        P(("tm", "rep"), "heads"),
        P(("tm", "rep"), "heads"),
        P(("tm", "rep"), "heads"),
        P(("tm", "rep"), None),
        P(("tm", "rep")),
        P("heads", "rep"),
        P("rep"),
    )
    return jax.shard_map(
        shards, mesh=mesh, in_specs=placed, out_specs=P(("tm", "heads"), "rep"), check_vma=False
    )
```

```python
import functools

import jax
import jax.numpy as jnp
from jax import lax
from jax.experimental import pallas as pl
from jax.experimental.pallas import tpu as pltpu
from jax.sharding import PartitionSpec as P

HD = 128
BLOCK = 128
LIST = 16
NEG = 1e30
MESH = pl.DeviceIdType.MESH


def extra_rep(g, reps):
    half = g // 2
    return ((1 - g % 2) * half + (g % 2) * (reps - 1 - half)) % reps


def kernel(
    dims,
    q_ref, k_ref, v_ref, lists_ref, counts_ref, w_ref,
    out_ref,
    qbuf, kbuf, vbuf, vturned, mbuf, stage, abuf, wbuf,
    zs, zr, zms, zmr, xs, xr, own_sem, w_own, ats, atr, gs, gr, wys, wyr, wxs, wxr, wms, wmr,
):
    frames, groups, reps, toks, heads, base, extra, parts = dims
    tm = lax.axis_index("tm")
    g = lax.axis_index("heads")
    z = lax.axis_index("rep")
    span = reps * toks
    local_blocks = toks // BLOCK
    frame_blocks = span // BLOCK
    part_rows = w_ref.shape[0] // parts
    halves = groups // 2

    def cols(head):
        return pl.ds(pl.multiple_of(head * HD, HD), HD)

    def rows(rep):
        return pl.ds(pl.multiple_of(rep * toks, toks), toks)

    def extra_rank(plane, group):
        return sum(
            jnp.where((other < group) & ((plane - extra_rep(other, reps) + reps) % reps < extra), 1, 0)
            for other in range(groups)
        )

    def extra_of(group):
        return (z - extra_rep(group, reps) + reps) % reps

    my_extra = extra_of(g)
    has_extra = my_extra < extra

    def extra_owner(plane, position):
        owner = sum(
            jnp.where(
                ((plane - extra_rep(other, reps) + reps) % reps < extra)
                & (extra_rank(plane, other) == position),
                other,
                0,
            )
            for other in range(groups)
        )
        return owner, base * reps + (plane - extra_rep(owner, reps) + reps) % reps

    barrier = pltpu.get_barrier_semaphore()
    for axis, count, me in (("rep", reps, z), ("tm", frames, tm), ("heads", groups, g)):
        for d in range(1, count):
            pl.semaphore_signal(
                barrier, inc=1, device_id={axis: (me + d) % count}, device_id_type=MESH
            )
    blocks = frames * frame_blocks
    key_block = lax.broadcasted_iota(jnp.int32, (blocks, toks), 0)
    query_block = lax.broadcasted_iota(jnp.int32, (blocks, toks), 1) // BLOCK
    term = jnp.full((blocks, toks), -NEG, jnp.float32)
    for b in range(local_blocks):
        used = counts_ref[b]
        for j in range(LIST):
            listed = jnp.where(j < used, lists_ref[b, j], -1)
            term = jnp.where((key_block == listed) & (query_block == b), 0.0, term)
    mbuf[z] = term
    pl.semaphore_wait(barrier, reps + frames + groups - 3)

    def mask_copy(dst, src):
        return pltpu.make_async_remote_copy(
            src_ref=mbuf.at[src], dst_ref=mbuf.at[src],
            send_sem=zms.at[dst], recv_sem=zmr.at[src],
            device_id={"rep": dst}, device_id_type=MESH,
        )

    sources = (k_ref, v_ref, q_ref)

    def landing(kind, slot, rep):
        if kind == 2:
            return qbuf.at[slot, rows(rep)]
        return (kbuf, vbuf)[kind].at[slot, tm, rows(rep)]

    def z_copy(kind, slot, head, dst, src):
        return pltpu.make_async_remote_copy(
            src_ref=sources[kind].at[:, cols(head)], dst_ref=landing(kind, slot, src),
            send_sem=zs.at[kind, slot, dst], recv_sem=zr.at[kind, slot, src],
            device_id={"rep": dst}, device_id_type=MESH,
        )

    def own_copy(kind, slot, head):
        return pltpu.make_async_copy(
            sources[kind].at[:, cols(head)], landing(kind, slot, z), own_sem.at[kind, slot]
        )

    def x_copy(kind, slot, rep, d, src=None):
        there = landing(kind, slot, rep)
        return pltpu.make_async_remote_copy(
            src_ref=there if src is None else src, dst_ref=there,
            send_sem=xs.at[kind, slot, rep, d - 1], recv_sem=xr.at[kind, slot, rep, d - 1],
            device_id={"tm": (tm + d) % frames}, device_id_type=MESH,
        )

    def my_head(slot):
        return slot * reps + z if slot < base else base * reps + my_extra

    def if_extra(act):
        if extra:
            pl.when(has_extra)(lambda: act(base))

    def each_base(act):
        for slot in range(base):
            act(slot)

    def start_own(kind, slot):
        if kind < 2:
            for d in range(1, frames):
                x_copy(kind, slot, z, d, sources[kind].at[:, cols(my_head(slot))]).start()
        own_copy(kind, slot, my_head(slot)).start()

    def wave(kind, d, act):
        dst = (z + d) % reps
        each_base(lambda slot: act(z_copy(kind, slot, slot * reps + dst, dst, z)))
        for n in range(extra):
            pl.when((extra_rep(g, reps) + n) % reps == dst)(
                lambda: act(z_copy(kind, base, base * reps + n, dst, z))
            )

    for d in range(1, reps):
        wave(0, d, lambda copy: copy.start())
    for kind in range(3):
        each_base(lambda slot: start_own(kind, slot))

    mate = g + 1 - 2 * (g % 2)
    pieces = parts

    def w_here(piece):
        return w_ref.at[pl.ds(piece * part_rows, part_rows)]

    def w_there(group, piece):
        return wbuf.at[group, pl.ds(piece * part_rows, part_rows)]

    def w_far(k, piece):
        return pltpu.make_async_remote_copy(
            src_ref=w_here(piece), dst_ref=w_there(g, piece),
            send_sem=wys.at[k - 1, piece], recv_sem=wyr.at[k - 1, piece],
            device_id={"heads": (g + 2 * k) % groups}, device_id_type=MESH,
        )

    def w_frame(k, piece, d):
        there = w_there((g - 2 * k + groups) % groups, piece)
        return pltpu.make_async_remote_copy(
            src_ref=there, dst_ref=there,
            send_sem=wxs.at[k - 1, piece, d - 1], recv_sem=wxr.at[k - 1, piece],
            device_id={"tm": (tm + d) % frames}, device_id_type=MESH,
        )

    def w_mate(k, piece):
        there = w_there((g - 2 * k + groups) % groups, piece)
        return pltpu.make_async_remote_copy(
            src_ref=there if k else w_here(piece), dst_ref=there,
            send_sem=wms.at[k, piece], recv_sem=wmr.at[k, piece],
            device_id={"heads": mate}, device_id_type=MESH,
        )

    def w_local(piece):
        return pltpu.make_async_copy(w_here(piece), w_there(g, piece), w_own.at[piece])

    def w_share(act, mine=True):
        for piece in range(pieces):
            fetch = tm == piece % frames

            @pl.when(fetch if mine else jnp.logical_not(fetch))
            def _():
                for k in range(1, halves):
                    act(k, piece)

    w_share(lambda k, piece: w_far(k, piece).start())

    for d in range(1, reps):
        mask_copy((z + d) % reps, z).start()

    for kind in range(3):
        if_extra(lambda slot: start_own(kind, slot))

    def pass_on(kind, src, slot):
        z_copy(kind, slot, 0, z, src).wait_recv()
        for e in range(1, frames):
            x_copy(kind, slot, src, e).start()

    def rest(slot):
        for kind in range(3):
            own_copy(kind, slot, my_head(slot)).wait()
        for kind in range(2):
            for rep in range(reps):
                for d in range(1, frames):
                    there = (kbuf, vbuf)[kind].at[slot, (tm - d + frames) % frames, rows(rep)]
                    pltpu.make_async_remote_copy(
                        src_ref=there, dst_ref=there,
                        send_sem=xs.at[kind, slot, rep, d - 1],
                        recv_sem=xr.at[kind, slot, rep, d - 1],
                        device_id={"tm": (tm + d) % frames}, device_id_type=MESH,
                    ).wait_recv()

    tile = min(span, 256)

    def turn_values(slot):
        def turn(frame, _):
            for at in range(0, span, tile):
                part = vbuf[slot, frame, at : at + tile].astype(jnp.float32)
                vturned[slot, frame, :, at : at + tile] = part.T.astype(jnp.bfloat16)
            return 0

        lax.fori_loop(0, frames, turn, 0)

    def attend(slot, chunk):
        queries = qbuf[slot, rows(chunk)]
        factor = 1.4426950408889634 / HD**0.5

        def step(frame, state):
            top, total, sums = state
            terms = mbuf[chunk, pl.ds(pl.multiple_of(frame * frame_blocks, frame_blocks), frame_blocks)]
            tiles = []
            new_top = top
            for at in range(0, span, tile):
                scores = lax.dot_general(
                    kbuf[slot, frame, at : at + tile], queries, (((1,), (1,)), ((), ())),
                    preferred_element_type=jnp.float32,
                )
                own_terms = terms[at // BLOCK : (at + tile) // BLOCK]
                scores = scores.reshape(tile // BLOCK, BLOCK, toks) + own_terms[:, None, :]
                scores = scores.reshape(tile, toks)
                new_top = jnp.maximum(new_top, jnp.max(scores, axis=0, keepdims=True))
                tiles.append(scores)
            scale = jnp.exp2((top - new_top) * factor)
            total = total * scale
            sums = sums * scale
            for n, scores in enumerate(tiles):
                weights = jnp.exp2((scores - new_top) * factor)
                total = total + jnp.sum(weights, axis=0, keepdims=True)
                sums = sums + jnp.dot(
                    vturned[slot, frame, :, n * tile : (n + 1) * tile],
                    weights.astype(jnp.bfloat16),
                    preferred_element_type=jnp.float32,
                )
            return new_top, total, sums

        state = (
            jnp.full((1, toks), -NEG, jnp.float32),
            jnp.zeros((1, toks), jnp.float32),
            jnp.zeros((HD, toks), jnp.float32),
        )
        _, total, sums = lax.fori_loop(0, frames, step, state, unroll=min(frames, 2))
        stage[slot, rows(chunk)] = (sums / total).T.astype(jnp.bfloat16)

    def position(slot, group):
        return slot * groups + group if slot < base else base * groups + extra_rank(z, group)

    def att_copy(slot, chunk):
        return pltpu.make_async_remote_copy(
            src_ref=stage.at[slot, rows(chunk)], dst_ref=abuf.at[z, :, cols(position(slot, g))],
            send_sem=ats.at[slot, chunk], recv_sem=atr.at[slot, g],
            device_id={"heads": chunk}, device_id_type=MESH,
        )

    def att_local(slot):
        return pltpu.make_async_copy(
            stage.at[slot, rows(g)], abuf.at[z, :, cols(position(slot, g))], ats.at[slot, g]
        )

    def arrive(slot, other):
        there = abuf.at[z, :, cols(position(slot, other))]
        pltpu.make_async_remote_copy(
            src_ref=stage.at[slot, rows(g)], dst_ref=there,
            send_sem=ats.at[slot, other], recv_sem=atr.at[slot, other],
            device_id={"heads": other}, device_id_type=MESH,
        ).wait_recv()

    def attend_all(slot, beside=lambda: None):
        def one_chunk(i, _):
            chunk = (z + i) % reps

            @pl.when(i > 0)
            def _():
                z_copy(2, slot, 0, z, chunk).wait_recv()

            attend(slot, chunk)

            @pl.when(chunk != g)
            def _():
                att_copy(slot, chunk).start()

            @pl.when(chunk == g)
            def _():
                att_local(slot).start()

            pl.when(i == max(reps - 2, 0))(beside)
            return 0

        turn_values(slot)
        lax.fori_loop(0, reps, one_chunk, 0)

    line_cols = (pl.ds(0, base * groups * HD), pl.ds(base * groups * HD, (heads - base * reps) * HD))
    line_parts = 2 if extra else 1

    def line_copy(part, src, way):
        there = abuf.at[src, :, line_cols[part]]
        return pltpu.make_async_remote_copy(
            src_ref=there, dst_ref=there,
            send_sem=gs.at[part, (way + 1) // 2, src], recv_sem=gr.at[part, src],
            device_id={"rep": (z + way + reps) % reps}, device_id_type=MESH,
        )

    def line_start(part):
        @pl.when(z + 1 < reps)
        def _():
            line_copy(part, z, 1).start()

        @pl.when(z > 0)
        def _():
            line_copy(part, z, -1).start()

    def line_relay(part, d):
        @pl.when(z - d >= 0)
        def _():
            src = (z - d + reps) % reps
            line_copy(part, src, 1).wait_recv()

            @pl.when(z + 1 < reps)
            def _():
                line_copy(part, src, 1).start()

        @pl.when(z + d < reps)
        def _():
            src = (z + d) % reps
            line_copy(part, src, -1).wait_recv()

            @pl.when(z > 0)
            def _():
                line_copy(part, src, -1).start()

    for kind in range(2):
        for d in range(1, reps):
            wave(kind, d, lambda copy: copy.wait_send())
            wave(kind + 1, d, lambda copy: copy.start())
        for d in range(1, reps):
            src = (z - d + reps) % reps
            each_base(lambda slot: pass_on(kind, src, slot))
            if_extra(lambda slot: pass_on(kind, src, slot))
    for piece in range(pieces):
        w_mate(0, piece).start()
        w_local(piece).start()

    for d in range(1, reps):
        mask_copy(z, (z + d) % reps).wait_recv()

    each_base(rest)

    def send_on(k, piece):
        w_far(k, piece).wait_recv()
        for d in range(1, frames):
            w_frame(k, piece, d).start()
        w_mate(k, piece).start()

    each_base(lambda slot: attend_all(slot, lambda: w_share(send_on) if slot == 0 else None))
    each_base(lambda slot: att_local(slot).wait())
    for d in range(1, groups):
        each_base(lambda slot: arrive(slot, (g + d) % groups))
    line_start(0)

    def to_mate(k, piece):
        w_frame(k, piece, 1).wait_recv()
        w_mate(k, piece).start()

    if_extra(rest)
    if_extra(attend_all)
    if extra:
        if_extra(lambda slot: att_local(slot).wait())
        for e in range(1, groups):
            other = (g + e) % groups
            pl.when(extra_of(other) < extra)(lambda: arrive(base, other))
        line_start(1)
    for d in range(1, reps - 1):
        for part in range(line_parts):
            line_relay(part, d)
    w_share(to_mate, mine=False)
    for piece in range(pieces):
        for k in range(halves):
            w_mate(k, piece).wait_recv()
        w_local(piece).wait()

    def product(src):
        total = None
        for at in range(abuf.shape[2] // HD):
            if at < base * groups:
                group, head = at % groups, (at // groups) * reps + src
            else:
                group, head = extra_owner(src, at - base * groups)
            term = jnp.dot(
                abuf[src, :, at * HD : (at + 1) * HD], wbuf[group, cols(head)],
                preferred_element_type=jnp.float32,
            )
            total = term if total is None else total + term
        return total

    out_ref[...] = product(z)
    for d in range(1, reps):
        if d == reps - 1:
            for part in range(line_parts):
                line_relay(part, d)

        @pl.when(z - d >= 0)
        def _():
            out_ref[...] += product((z - d + reps) % reps)

        @pl.when(z + d < reps)
        def _():
            out_ref[...] += product((z + d) % reps)

    for d in range(1, reps):
        mask_copy((z + d) % reps, z).wait_send()
        wave(2, d, lambda copy: copy.wait_send())

    def sent(slot):
        for kind in range(2):
            for rep in range(reps):
                for d in range(1, frames):
                    x_copy(kind, slot, rep, d).wait_send()
        for d in range(1, groups):
            att_copy(slot, (g + d) % groups).wait_send()

    each_base(sent)
    if_extra(sent)

    def share_sent(k, piece):
        w_far(k, piece).wait_send()
        for d in range(1, frames):
            w_frame(k, piece, d).wait_send()

    w_share(share_sent)
    for piece in range(pieces):
        for k in range(halves):
            w_mate(k, piece).wait_send()

    for part in range(line_parts):
        @pl.when(z + 1 < reps)
        def _():
            for src in range(reps):
                pl.when(src <= z)(lambda: line_copy(part, src, 1).wait_send())

        @pl.when(z > 0)
        def _():
            for src in range(reps):
                pl.when(src >= z)(lambda: line_copy(part, src, -1).wait_send())


def shards(queries, keys, values, block_lists, list_counts, out_weight, gate):
    frames, groups, reps = (lax.axis_size(a) for a in ("tm", "heads", "rep"))
    toks = queries.shape[0]
    heads = queries.shape[1] // HD
    wide = out_weight.shape[1]
    base, extra = heads // reps, heads % reps
    slots = base + (1 if extra else 0)
    assert groups == reps and groups % 2 == 0
    plane_heads = heads * groups // reps
    span = reps * toks
    parts = 2 if out_weight.shape[0] % 32 == 0 else 1
    dims = (frames, groups, reps, toks, heads, base, extra, parts)
    others = max(frames - 1, 1)
    halves = groups // 2
    far = max(halves - 1, 1)
    pieces = parts
    vmem, smem, hbm = (
        pl.BlockSpec(memory_space=m) for m in (pltpu.VMEM, pltpu.SMEM, pl.ANY)
    )
    dma = pltpu.SemaphoreType.DMA
    scores = slots * span * span * frames
    summed = pl.pallas_call(
        functools.partial(kernel, dims),
        out_shape=jax.ShapeDtypeStruct((toks, wide), jnp.float32),
        in_specs=[hbm, hbm, hbm, smem, smem, hbm],
        out_specs=vmem,
        scratch_shapes=[
            pltpu.VMEM((slots, span, HD), jnp.bfloat16),
            pltpu.VMEM((slots, frames, span, HD), jnp.bfloat16),
            pltpu.VMEM((slots, frames, span, HD), jnp.bfloat16),
            pltpu.VMEM((slots, frames, HD, span), jnp.bfloat16),
            pltpu.VMEM((reps, span * frames // BLOCK, toks), jnp.float32),
            pltpu.VMEM((slots, span, HD), jnp.bfloat16),
            pltpu.VMEM((reps, toks, plane_heads * HD), jnp.bfloat16),
            pltpu.VMEM((groups, heads * HD, wide), jnp.bfloat16),
            dma((3, slots, reps)), dma((3, slots, reps)),
            dma((reps,)), dma((reps,)),
            dma((2, slots, reps, others)), dma((2, slots, reps, others)),
            dma((3, slots)), dma((pieces,)),
            dma((slots, groups)), dma((slots, groups)),
            dma((2, 2, reps)), dma((2, reps)),
            dma((far, pieces)), dma((far, pieces)),
            dma((far, pieces, others)), dma((far, pieces)),
            dma((halves, pieces)), dma((halves, pieces)),
        ],
        compiler_params=pltpu.CompilerParams(
            collective_id=0, has_side_effects=True, vmem_limit_bytes=56 * 2**20
        ),
        cost_estimate=pl.CostEstimate(
            flops=4 * scores * HD + 2 * toks * plane_heads * HD * reps * wide,
            bytes_accessed=2 * (3 * queries.size + out_weight.size),
            transcendentals=scores,
        ),
    )(queries, keys, values, block_lists, list_counts, out_weight)
    return (gate[None, :] * summed).astype(jnp.bfloat16)


def solution(mesh):
    placed = (
        P(("tm", "rep"), "heads"),
        P(("tm", "rep"), "heads"),
        P(("tm", "rep"), "heads"),
        P(("tm", "rep"), None),
        P(("tm", "rep")),
        P("heads", "rep"),
        P("rep"),
    )
    return jax.shard_map(
        shards, mesh=mesh, in_specs=placed, out_specs=P(("tm", "heads"), "rep"), check_vma=False
    )
```
